256 devices in a mesh: outer: 16 (over x, y), inner: 4 (over z_hi, core), cell: 4 (over z_lo).
Axes of the slice: x: 4, y: 4, z: 8 (z_hi: 2, z_lo: 4; z = z_hi * 4 + z_lo), core: 2. Of those that a mesh axis runs over, the one named last changes fastest.
Arguments:
- premium: float32 [48, 8192], P('outer', 'cell'), may hold values from 0.1 to 1
- charge: float32 [48, 8192], P('outer', 'cell'), may hold values from 0.05 to 2
- mortality: float32 [48, 8192], P('outer', 'cell'), may hold values from 0.0005 to 0.01
- lapse_table: float32 [16, 48], replicated, may hold values from 0.001 to 0.02
- lapse_index: int32 [8192], P('cell'), may hold values from 0 to 15
- guarantee_type: int32 [8192], P('cell'), may hold values from 0 to 2
- block_index: int32 [8192], P('cell'), may hold values from 0 to 255, never falling along the last dimension, each value on 1 to 128 neighbouring positions
- account_start: float32 [8192], P('cell'), may hold values from 5 to 50
- guarantee_start: float32 [8192], P('cell'), may hold values from 5 to 60
- fee_rate: float32 [8192], P('cell'), may hold values from 0.0003 to 0.002
- first_rates: float32 [64, 64, 36], P('outer', 'inner'), may hold values from 0 to 0.006
- second_rates: float32 [64, 64, 24], P('outer', 'inner'), may hold values from 0 to 0.006
- world_rates: float32 [64, 24], P('outer'), may hold values from 0 to 0.006
- spread: float32 [64], P('outer'), may hold values from 0.0005 to 0.002
Outputs:
- cell_reserve: float32 [2, 64, 8192], P(None, ('outer', 'inner'), 'cell')
- block_reserve: float32 [2, 64, 256], P(None, ('outer', 'inner'), 'cell')
- capital: float32 [1], replicated
The draws below stay inside these ranges and needn't reach their ends.
Inputs may be any that keep to these rules, and one draw needn't show every extreme that they name: `block_index`: block numbers never fall along the cells; every block holds 1 to 128 cells.
All inputs are finite; a program needn't handle non-finite values.
Results may differ from the reference program's by a relative error of at most 0.0003.
Values sent between devices are 32-bit elements; how exact they have to be, the bound alone decides.
No kernel may reach another device: no remote copies, remote signals or barrier semaphores. Data moves between devices by JAX's collectives and lax.ppermute only.
A program may use at most 64 MiB of HBM per device.

```python
import math
import jax
import jax.numpy as jnp
import numpy as np
from jax import lax

PERIOD = 12
BLOCK = 128
LAPSE_TABLES = 16
MONTHS = 48
OUTER = 64
PATHS = 64
CELLS = 8192
NBLK = 256


def rate_paths(key, months):
    level_key, shock_key = jax.random.split(key, 2)
    level = jax.random.uniform(level_key, (OUTER, PATHS, 1), jnp.float32, 0.0, 0.006)
    shocks = 0.0004 * jax.random.normal(shock_key, (OUTER, PATHS, months), jnp.float32)
    walked = level + jnp.cumsum(shocks, axis=2)
    return jnp.clip(walked, 0.0, 0.006)


def draw_first_rates(key, part):
    return rate_paths(jax.random.fold_in(key, 11), MONTHS - PERIOD)


def draw_second_rates(key, part):
    return rate_paths(jax.random.fold_in(key, 12), MONTHS - 2 * PERIOD)


def draw_charge(key, part):
    group_key, value_key = jax.random.split(jax.random.fold_in(key, 21))
    heavy = jax.random.uniform(group_key, (1, CELLS), jnp.float32) < 0.125
    unit = jax.random.uniform(value_key, (MONTHS, CELLS), jnp.float32)
    light = 0.05 * jnp.exp(unit * math.log(10.0))
    dense = jnp.exp(unit * math.log(2.0))
    return jnp.where(heavy, dense, light)


def with_ends(values, rng, least, largest):
    index_at = [jax.random.randint(jax.random.fold_in(rng, axis), (), 0, length) for axis, length in enumerate(values.shape)]
    widest = values.shape.index(max(values.shape))
    beside = index_at[:widest] + [(index_at[widest] + 1) % values.shape[widest]] + index_at[widest + 1:]
    return values.at[tuple(index_at)].set(least).at[tuple(beside)].set(largest)


def block_levels(rng, shape, cuts, low, largest):
    gain, own = 1.0, jax.random.fold_in(rng, 6)
    for dim, blocks in cuts:
        heights = jnp.exp(jax.random.uniform(jax.random.fold_in(own, dim), (blocks,), jnp.float32, low / len(cuts), largest / len(cuts)))
        gain = gain * jnp.repeat(heights, shape[dim] // blocks).reshape([-1 if axis == dim else 1 for axis in range(len(shape))])
    return gain


def profile(number_of, total, limit, lean):
    weights = [(1 << 20) // math.isqrt(standing ** lean) + 1 for standing in range(2, number_of + 1)]
    spare, given = total - limit - (number_of - 1), [1] * (number_of - 1)
    while spare > 0:
        candidates = [i for i in range(number_of - 1) if given[i] < limit]
        mass, budget = sum([weights[i] for i in candidates]), spare
        for i in candidates:
            addition = min(limit - given[i], max(1, budget * weights[i] // mass), spare)
            given[i] = given[i] + addition
            spare = spare - addition
    return np.array([limit] + given)


def uneven_parts(stream_key, count, total, limit, skew):
    if count == 2:
        one = jax.random.randint(stream_key, (), max(1, total - limit), min(limit, total - 1) + 1)
        return jnp.stack([one, total - one])
    sizes = jnp.asarray(profile(count, total, limit, skew), jnp.int32)
    pairs = (count - 1) // 2
    donor, sink = sizes[1:1 + 2 * pairs:2], sizes[2:2 + 2 * pairs:2]
    slack = jnp.minimum(donor - 1, limit - sink)
    shifted = jax.random.randint(jax.random.fold_in(stream_key, 1), (pairs,), 0, 1 << 20) % (slack + 1)
    sizes = sizes.at[1:1 + 2 * pairs:2].set(donor - shifted).at[2:2 + 2 * pairs:2].set(sink + shifted)
    return sizes[jax.random.permutation(jax.random.fold_in(stream_key, 2), count)]


def setup_inputs(seed: int = 0) -> dict:
    key_of = jax.random.split(jax.random.key(seed), 15)
    return {
        "premium": jnp.clip(jnp.exp(math.log(1.0) - 2.3025851 * jax.random.uniform(key_of[0], (MONTHS, CELLS), jnp.float32) ** block_levels(key_of[0], (MONTHS, CELLS), ((0, 16), (1, 4)), -0.2, 0.2)), 0.1, 1.0),
        "charge": draw_charge(jax.random.fold_in(key_of[14], 71), 0),
        "mortality": jnp.clip(jnp.exp(math.log(0.01) - 2.9957322 * jax.random.uniform(key_of[2], (MONTHS, CELLS), jnp.float32) ** block_levels(key_of[2], (MONTHS, CELLS), ((0, 16), (1, 4)), -0.2, 0.2)), 0.0005, 0.01),
        "lapse_table": jnp.clip(jnp.exp(jax.random.uniform(key_of[3], (LAPSE_TABLES, MONTHS), jnp.float32, math.log(0.001), math.log(0.02))), 0.001, 0.02),
        "lapse_index": with_ends(jax.random.randint(key_of[4], (CELLS,), 0, LAPSE_TABLES), jax.random.fold_in(key_of[4], 1), 0, LAPSE_TABLES - 1).astype(jnp.int32),
        "guarantee_type": with_ends(jax.random.randint(key_of[5], (CELLS,), 0, 3), jax.random.fold_in(key_of[5], 1), 0, 2).astype(jnp.int32),
        "block_index": jnp.searchsorted(jnp.cumsum(uneven_parts(key_of[6], NBLK, CELLS, BLOCK, 1)), jnp.arange(CELLS), side="right").astype(jnp.int32),
        "account_start": jnp.clip(jnp.exp(math.log(50.0) - 2.3025851 * jax.random.uniform(key_of[7], (CELLS,), jnp.float32) ** block_levels(key_of[7], (CELLS,), ((0, 4),), -0.2, 0.2)), 5.0, 50.0),
        "guarantee_start": jnp.clip(jnp.exp(math.log(60.0) - 2.4849066 * jax.random.uniform(key_of[8], (CELLS,), jnp.float32) ** block_levels(key_of[8], (CELLS,), ((0, 4),), -0.2, 0.2)), 5.0, 60.0),
        "fee_rate": jnp.clip(jnp.exp(math.log(0.002) - 1.89712 * jax.random.uniform(key_of[9], (CELLS,), jnp.float32) ** block_levels(key_of[9], (CELLS,), ((0, 4),), -0.2, 0.2)), 0.0003, 0.002),
        "first_rates": draw_first_rates(jax.random.fold_in(key_of[14], 71), 0),
        "second_rates": draw_second_rates(jax.random.fold_in(key_of[14], 71), 0),
        "world_rates": jnp.clip(0.006 * jax.random.uniform(key_of[12], (OUTER, 2 * PERIOD), jnp.float32) ** block_levels(key_of[12], (OUTER, 2 * PERIOD), ((0, 16),), -0.2, 0.2), 0.0, 0.006),
        "spread": jnp.clip(0.0005 + 0.0015 * jax.random.uniform(key_of[13], (OUTER,), jnp.float32) ** block_levels(key_of[13], (OUTER,), ((0, 16),), -0.2, 0.2), 0.0005, 0.002),
    }


credit_floor = 0.001
rollup_growth = 0.05


def month_step(account, surviving, guarantee, log_discount, present, short_rate, net_flow, mortality, lapse_base, fee_rate, spread):
    rider_fee = fee_rate * account
    before = jnp.maximum(account + net_flow - rider_fee, 0.0)
    credited = before * (1.0 + jnp.maximum(short_rate - spread, credit_floor))
    log_discount = log_discount + short_rate
    lapse_rate = lapse_base * jnp.clip(credited / guarantee, 0.5, 1.5)
    claims = surviving * (mortality * jnp.maximum(guarantee - credited, 0.0) - rider_fee)
    present = present + jnp.exp(-log_discount) * claims
    surviving = surviving * (1.0 - mortality - lapse_rate)
    return credited, surviving, log_discount, present


def anniversary(account, guarantee, ratchet, rollup):
    return guarantee + ratchet * (jnp.maximum(guarantee, account) - guarantee) + rollup * rollup_growth * guarantee


def project_ref(account, surviving, guarantee, short_rates, start_month, spread, plans, fee_rate, ratchet, rollup):
    net_flow, mortality, lapse_base = plans
    log_discount = jnp.zeros((short_rates.shape[0], 1), jnp.float32)
    present = jnp.zeros((1, 1), jnp.float32)
    for offset in range(short_rates.shape[1]):
        calendar = start_month + offset
        account, surviving, log_discount, present = month_step(
            account, surviving, guarantee, log_discount, present, short_rates[:, offset:offset + 1],
            net_flow[calendar], mortality[calendar], lapse_base[calendar], fee_rate, spread)
        if (calendar + 1) % PERIOD == 0:
            guarantee = anniversary(account, guarantee, ratchet, rollup)
    return account, surviving, guarantee, present


def reference(premium, charge, mortality, lapse_table, lapse_index, guarantee_type, block_index, account_start, guarantee_start, fee_rate, first_rates, second_rates, world_rates, spread):
    net_flow = premium - charge
    lapse_base = lapse_table[lapse_index].T
    plans = (net_flow, mortality, lapse_base)
    ratchet = (guarantee_type == 1).astype(jnp.float32)
    rollup = (guarantee_type == 2).astype(jnp.float32)

    def one_outer(inputs):
        rates_one, rates_two, world_one, spread_one = inputs
        world_row = world_one[None, :]
        year_one = project_ref(account_start[None, :], jnp.ones((1, CELLS), jnp.float32), guarantee_start[None, :],
                               world_row[:, :PERIOD], 0, spread_one, plans, fee_rate, ratchet, rollup)
        inner_one = project_ref(year_one[0], year_one[1], year_one[2], rates_one, PERIOD, spread_one,
                                plans, fee_rate, ratchet, rollup)
        reserve_one = jnp.sum(inner_one[3], axis=0) / PATHS
        total_one = jnp.sum(reserve_one)
        spread_two = spread_one * (1.0 + jnp.tanh(total_one / CELLS))
        year_two = project_ref(year_one[0], year_one[1], year_one[2], world_row[:, PERIOD:], PERIOD, spread_two,
                               plans, fee_rate, ratchet, rollup)
        inner_two = project_ref(year_two[0], year_two[1], year_two[2], rates_two, 2 * PERIOD, spread_two,
                                plans, fee_rate, ratchet, rollup)
        reserve_two = jnp.sum(inner_two[3], axis=0) / PATHS
        total_two = jnp.sum(reserve_two)
        discount = jnp.exp(-jnp.sum(world_one[PERIOD:]))
        outer_loss = (discount * total_two - total_one) / CELLS
        return jnp.stack([reserve_one, reserve_two]), outer_loss

    reserves, losses = lax.map(one_outer, (first_rates, second_rates, world_rates, spread))
    cell_reserve = jnp.transpose(reserves, (1, 0, 2))
    block_hot = (block_index[:, None] == jnp.arange(NBLK)[None, :]).astype(jnp.float32)
    block_reserve = jnp.dot(cell_reserve.reshape(2 * OUTER, CELLS), block_hot,
                            precision=lax.Precision.HIGHEST).reshape(2, OUTER, NBLK)
    ordered = jnp.sort(losses)
    capital = jnp.mean(ordered[OUTER - OUTER // 4:]).reshape((1,))
    return cell_reserve, block_reserve, capital
```

```python
import functools

import jax
import jax.numpy as jnp
from jax import lax
from jax.experimental import pallas as pl
from jax.experimental.pallas import tpu as pltpu
from jax.sharding import PartitionSpec as P

PERIOD = 12
LANES = 128
SUBLANES = 8

credit_floor = 0.001
rollup_growth = 0.05
ALL = ("outer", "inner", "cell")

FEE, KEPT, ACCOUNT, GUARANTEE, RATCHET, ROLLUP = range(6)
S_ACCOUNT, S_SURVIVING, S_GUARANTEE = range(3)


def row_of(month, each):
    return month // each, month % each


def world_year(start, each, plan, level, low, high, lapse, cells, state, credit):
    fee, kept = cells[FEE : FEE + 1, :], cells[KEPT : KEPT + 1, :]
    ratchet, rollup = cells[RATCHET : RATCHET + 1, :], cells[ROLLUP : ROLLUP + 1, :]
    account, surviving, guarantee = state
    per_guarantee = 1.0 / guarantee
    for m in range(start, start + PERIOD):
        d, r = row_of(m, each)
        flow = plan[d, r : r + 1, :]
        death = plan[d, each + r : each + r + 1, :]
        account = jnp.maximum(account + flow * per_guarantee, 0.0) * credit(m)
        bounded = jnp.minimum(jnp.maximum(account, low[m : m + 1, :]), high[m : m + 1, :])
        surviving = surviving * (kept - fee * death - lapse[m : m + 1, :] * bounded)
    unit = level[start + PERIOD - 1 : start + PERIOD, :]
    growth = jnp.maximum(ratchet * (account / unit), 1.0 + rollup_growth * rollup)
    account = jnp.where(ratchet > 0.5, jnp.minimum(account, unit), account / growth)
    return account, surviving, guarantee * growth


def inner_paths(
    start, months, each, plan, level, low, high, lapse, cells, rows, credit, discount, kept_accounts, kept_growth, reserve
):
    groups = credit.shape[1] // SUBLANES
    paths = credit.shape[1]
    years = months // PERIOD

    def tile_step(t, total):
        tile = pl.ds(pl.multiple_of(t * LANES, LANES), LANES)

        def spread_out(ref, r):
            return jnp.broadcast_to(ref[pl.ds(r, 1), tile], (SUBLANES, LANES))

        def planned(m, second):
            d, r = row_of(m, each)
            return jnp.broadcast_to(plan[d, pl.ds(r + second * each, 1), tile], (SUBLANES, LANES))

        def group(ref, m, g):
            return ref[m, SUBLANES * g : SUBLANES * (g + 1), :]

        fee, kept = spread_out(cells, FEE), spread_out(cells, KEPT)
        ratchet, rollup = spread_out(cells, RATCHET), spread_out(cells, ROLLUP)
        grown = 1.0 + rollup_growth * rollup
        shrunk = 1.0 / grown
        begin = spread_out(rows, S_ACCOUNT)
        guarantee = spread_out(rows, S_GUARANTEE)
        base = 1.0 / guarantee
        account = [begin] * groups
        per_guarantee = [base] * groups
        for y in range(years):
            for s in range(PERIOD):
                o = y * PERIOD + s
                flow = planned(start + o, 0)
                if y == 0:
                    flow = flow * base
                for g in range(groups):
                    term = flow if y == 0 else flow * per_guarantee[g]
                    account[g] = jnp.maximum(account[g] + term, 0.0) * group(credit, o, g)
                    kept_accounts[o, SUBLANES * g : SUBLANES * (g + 1), :] = account[g]
            if y + 1 < years:
                unit = spread_out(level, start + y * PERIOD + PERIOD - 1)
                per_unit = ratchet / unit
                cap = jnp.where(ratchet > 0.5, unit, 1e30)
                for g in range(groups):
                    growth = jnp.maximum(per_unit * account[g], grown)
                    kept_growth[y, SUBLANES * g : SUBLANES * (g + 1), :] = growth
                    per_guarantee[g] = per_guarantee[g] / growth
                    account[g] = jnp.minimum(account[g], cap) * shrunk
                    kept_growth[years + y, SUBLANES * g : SUBLANES * (g + 1), :] = account[g]
        worth = [None] * groups
        for o in reversed(range(months)):
            m = start + o
            unit, least, most = spread_out(level, m), spread_out(low, m), spread_out(high, m)
            lapsing = spread_out(lapse, m)
            death = planned(m, 1)
            staying = kept - fee * death
            for g in range(groups):
                after = group(kept_accounts, o, g)
                if o == 0:
                    before = begin
                elif o % PERIOD == 0:
                    before = group(kept_growth, years + o // PERIOD - 1, g)
                else:
                    before = group(kept_accounts, o - 1, g)
                value = death * jnp.maximum(unit - after, 0.0) - before
                if worth[g] is not None:
                    later = worth[g]
                    if (o + 1) % PERIOD == 0:
                        later = later * group(kept_growth, o // PERIOD, g)
                    bounded = jnp.minimum(jnp.maximum(after, least), most)
                    value = value + (staying - lapsing * bounded) * later
                worth[g] = value * group(discount, o, g)
        summed = worth[0]
        for g in range(1, groups):
            summed = summed + worth[g]
        scale = guarantee * spread_out(rows, S_SURVIVING) * (1.0 / paths)
        row = jnp.sum(summed * scale, axis=0, keepdims=True)
        reserve[0:1, tile] = row
        return total + row

    tiles = reserve.shape[1] // LANES
    return lax.fori_loop(0, tiles, tile_step, jnp.zeros((1, LANES), jnp.float32))


def first_kernel(
    each, credit_world, spread, plan, level, low, high, lapse, cells, rates,
    reserve, rows, total, credit, discount, kept_accounts, kept_growth,
):
    months = credit.shape[0]
    crediting = 1.0 + jnp.maximum(rates[...] - spread[0], credit_floor)
    discounting = jnp.exp(-rates[...])
    for m in range(months):
        credit[m] = jnp.broadcast_to(crediting[:, m : m + 1], credit.shape[1:])
        discount[m] = jnp.broadcast_to(discounting[:, m : m + 1], credit.shape[1:])
    fee, guarantee = cells[FEE : FEE + 1, :], cells[GUARANTEE : GUARANTEE + 1, :]
    account = fee * cells[ACCOUNT : ACCOUNT + 1, :] / guarantee
    state = (account, jnp.ones_like(account), guarantee)
    state = world_year(0, each, plan, level, low, high, lapse, cells, state, lambda m: credit_world[m])
    for r, value in enumerate(state):
        rows[r : r + 1, :] = value
    total[...] = inner_paths(
        PERIOD, months, each, plan, level, low, high, lapse, cells, rows, credit, discount, kept_accounts, kept_growth, reserve
    )


def second_kernel(
    each, cells_all, block_count, world, spread, place, total_one, next_one, next_two, next_three,
    plan, level, low, high, lapse, cells, rates, rows_one, reserve_one, block_hot,
    reserves, parcel, rows, reserve, credit, discount, kept_accounts, kept_growth, parts,
):
    months = credit.shape[0]
    whole = total_one[...] + next_one[...] + next_two[...] + next_three[...]
    mean = jnp.broadcast_to(jnp.sum(whole, axis=1, keepdims=True), (1, LANES)) / cells_all
    spread_two = (spread[0] * (1.0 + jnp.tanh(mean)))[0, 0]
    crediting = 1.0 + jnp.maximum(rates[...] - spread_two, credit_floor)
    discounting = jnp.exp(-rates[...])
    first = rates.shape[1] - months
    for m in range(months):
        credit[m] = jnp.broadcast_to(crediting[:, first + m : first + m + 1], credit.shape[1:])
        discount[m] = jnp.broadcast_to(discounting[:, first + m : first + m + 1], credit.shape[1:])
    state = tuple(rows_one[r : r + 1, :] for r in range(3))
    state = world_year(
        PERIOD, each, plan, level, low, high, lapse, cells, state,
        lambda m: 1.0 + jnp.maximum(world[m] - spread_two, credit_floor),
    )
    for r, value in enumerate(state):
        rows[r : r + 1, :] = value
    total_two = inner_paths(
        2 * PERIOD, months, each, plan, level, low, high, lapse, cells, rows, credit, discount, kept_accounts, kept_growth, reserve
    )
    parts[...] = jnp.zeros_like(parts)
    for d, source in enumerate((reserve_one, reserve)):
        value = source[0:1, :]
        reserves[d] = value
        for part in range(3):
            rounded = value.astype(jnp.bfloat16).astype(jnp.float32)
            parts[3 * d + part : 3 * d + part + 1, :] = rounded
            value = value - rounded
    sums = jnp.dot(parts[...].astype(jnp.bfloat16), block_hot[...], preferred_element_type=jnp.float32)
    first_sums = sums[0:1, :] + sums[1:2, :] + sums[2:3, :]
    second_sums = sums[3:4, :] + sums[4:5, :] + sums[5:6, :]
    rate_sum = world[PERIOD]
    for m in range(PERIOD + 1, 2 * PERIOD):
        rate_sum = rate_sum + world[m]
    discount_world = jnp.exp(jnp.full((1, LANES), -rate_sum, jnp.float32))
    local = discount_world * total_two - total_one[...]
    loss = jnp.broadcast_to(jnp.sum(local, axis=1, keepdims=True), (1, LANES)) / cells_all
    lane = lax.broadcasted_iota(jnp.int32, (1, LANES), 1)
    loss = jnp.where(lane == place[0], loss, 0.0)
    owners = parcel.shape[1]
    kept = block_count // owners
    for k in range(owners):
        blocks = jnp.concatenate(
            [first_sums[:, kept * k : kept * (k + 1)], second_sums[:, kept * k : kept * (k + 1)]], axis=1
        )
        both = jnp.concatenate([blocks, loss], axis=0)
        parcel[:, k] = jnp.broadcast_to(both[None], (parcel.shape[0], 2, LANES))


def last_kernel(place, received, block_reserve, capital):
    outers, owners = received.shape[0], received.shape[1]
    losses = received[:, 0, 1, :]
    for k in range(1, owners):
        losses = losses + received[:, k, 1, :]
    across = jnp.sum(losses, axis=0, keepdims=True)
    down = jnp.sum(losses, axis=1, keepdims=True)
    lane = lax.broadcasted_iota(jnp.int32, losses.shape, 1)
    place_down = lax.broadcasted_iota(jnp.int32, losses.shape, 0)
    ahead = (across > down) | ((across == down) & (lane < place_down))
    ahead = ahead & (lane < outers)
    rank = jnp.sum(jnp.where(ahead, 1.0, 0.0), axis=1, keepdims=True)
    count_top = outers // 4
    chosen = jnp.where(rank < count_top - 0.5, down, 0.0)
    capital[...] = jnp.broadcast_to(jnp.sum(chosen, axis=0, keepdims=True) / count_top, capital.shape)
    blocks = received[place[0], 0, 0:1, :]
    for k in range(1, owners):
        blocks = blocks + received[place[0], k, 0:1, :]
    kept = block_reserve.shape[2]
    for d in range(2):
        block_reserve[d] = blocks[:, kept * d : kept * (d + 1)]


VMEM = pl.BlockSpec(memory_space=pltpu.VMEM)
SMEM = pl.BlockSpec(memory_space=pltpu.SMEM)
LIMIT = pltpu.CompilerParams(vmem_limit_bytes=48 * 1024 * 1024)


def body(
    premium,
    charge,
    mortality,
    lapse_table,
    lapse_index,
    guarantee_type,
    block_index,
    account_start,
    guarantee_start,
    fee_rate,
    first_rates,
    second_rates,
    world_rates,
    spread,
):
    f32 = jnp.float32
    outer_size, inner_size, cell_size = (lax.axis_size(a) for a in ALL)
    each, local = premium.shape
    months_all = each * outer_size
    inner_at = lax.axis_index("inner")
    place = lax.axis_index("outer") * inner_size + inner_at
    paths = first_rates.shape[1] * inner_size
    months_one, months_two = first_rates.shape[2], second_rates.shape[2]
    cells_all = local * cell_size
    block_count = 4 * cells_all // LANES

    fee = fee_rate[None, :]
    fee_log = jnp.log1p(-fee)

    def scale_of(month):
        return fee * jnp.exp(-(month.astype(f32)[:, None] + 1.0) * fee_log)

    own_months = lax.axis_index("outer") * each + jnp.arange(each)
    flow = (premium - charge) * scale_of(own_months)
    death = mortality * ((1.0 - fee) / fee)
    sent = jnp.concatenate([flow, death], axis=0)
    sent = jnp.broadcast_to(sent[None], (outer_size, *sent.shape))
    plan = lax.all_to_all(sent, "outer", 0, 0, tiled=True)
    rates = lax.all_to_all(jnp.concatenate([first_rates, second_rates], axis=2), "inner", 0, 0, tiled=True)
    rates = rates.reshape(paths, months_one + months_two)

    level = scale_of(jnp.arange(months_all))
    tables = jnp.arange(lapse_table.shape[0])
    lapse_hot = (lapse_index[None, :] == tables[:, None]).astype(f32)
    lapse = jnp.dot(lapse_table.T, lapse_hot, precision=lax.Precision.HIGHEST) * ((1.0 - fee) / level)
    low, high = 0.5 * level, 1.5 * level
    cells = jnp.stack(
        [
            fee_rate,
            1.0 - fee_rate,
            account_start,
            guarantee_start,
            (guarantee_type == 1).astype(f32),
            (guarantee_type == 2).astype(f32),
        ]
    )
    world = lax.dynamic_index_in_dim(world_rates, inner_at, 0, False)
    spread_own = lax.dynamic_slice_in_dim(spread, inner_at, 1, 0)
    credit_world = 1.0 + jnp.maximum(world - spread_own, credit_floor)
    place_own = place.astype(jnp.int32).reshape(1)
    block_hot = (block_index[:, None] == jnp.arange(block_count)[None, :]).astype(jnp.bfloat16)

    row = jax.ShapeDtypeStruct((1, local), f32)

    def inner_scratch(months):
        years = months // PERIOD
        return [
            pltpu.VMEM((months, paths, LANES), f32),
            pltpu.VMEM((months, paths, LANES), f32),
            pltpu.VMEM((months, paths, LANES), f32),
            pltpu.VMEM((2 * years, paths, LANES), f32),
        ]

    reserve_one, rows_one, total_one = pl.pallas_call(
        functools.partial(first_kernel, each),
        out_shape=(row, jax.ShapeDtypeStruct((3, local), f32), jax.ShapeDtypeStruct((1, LANES), f32)),
        in_specs=[SMEM] * 2 + [VMEM] * 7,
        out_specs=[VMEM] * 3,
        scratch_shapes=inner_scratch(months_one),
        compiler_params=LIMIT,
        name="first_date",
    )(credit_world, spread_own, plan, level, low, high, lapse, cells, rates)

    others = [
        lax.ppermute(total_one, "cell", [(k, (k + s) % cell_size) for k in range(cell_size)])
        for s in range(1, cell_size)
    ]

    reserves, parcel = pl.pallas_call(
        functools.partial(second_kernel, each, cells_all, block_count),
        out_shape=(
            jax.ShapeDtypeStruct((2, 1, local), f32),
            jax.ShapeDtypeStruct((outer_size * inner_size, cell_size, 2, LANES), f32),
        ),
        in_specs=[SMEM] * 3 + [VMEM] * 14,
        out_specs=[VMEM] * 2,
        scratch_shapes=[pltpu.VMEM((3, local), f32), pltpu.VMEM((1, local), f32)]
        + inner_scratch(months_two)
        + [pltpu.VMEM((SUBLANES, local), f32)],
        compiler_params=LIMIT,
        name="second_date",
    )(
        world, spread_own, place_own, total_one, *others,
        plan, level, low, high, lapse, cells, rates, rows_one, reserve_one, block_hot,
    )

    received = lax.all_to_all(parcel.reshape(-1, 2, LANES), ALL, 0, 0, tiled=True)
    block_reserve, capital = pl.pallas_call(
        last_kernel,
        out_shape=(
            jax.ShapeDtypeStruct((2, 1, block_count // cell_size), f32),
            jax.ShapeDtypeStruct((1, LANES), f32),
        ),
        in_specs=[SMEM, VMEM],
        out_specs=[VMEM] * 2,
        compiler_params=LIMIT,
        name="last_sums",
    )(place_own, received.reshape(parcel.shape))
    return reserves, block_reserve, capital[0, :1]


def solution(mesh):
    placed = (
        P("outer", "cell"),
        P("outer", "cell"),
        P("outer", "cell"),
        P(),
        P("cell"),
        P("cell"),
        P("cell"),
        P("cell"),
        P("cell"),
        P("cell"),
        P("outer", "inner", None),
        P("outer", "inner", None),
        P("outer", None),
        P("outer"),
    )
    return jax.shard_map(
        body,
        mesh=mesh,
        in_specs=placed,
        out_specs=(P(None, ("outer", "inner"), "cell"), P(None, ("outer", "inner"), "cell"), P()),
        check_vma=False,
    )
```

```python
import functools

import jax
import jax.numpy as jnp
from jax import lax
from jax.experimental import pallas as pl
from jax.experimental.pallas import tpu as pltpu
from jax.sharding import PartitionSpec as P

PERIOD = 12
LANES = 128
SUBLANES = 8

credit_floor = 0.001
rollup_growth = 0.05
ALL = ("outer", "inner", "cell")

FEE, ACCOUNT, GUARANTEE, RATCHET, ROLLUP = range(5)
S_ACCOUNT, S_SURVIVING, S_GUARANTEE = range(3)


def lines_of(month, count):
    return slice(month * count, (month + 1) * count)


def parcel_kernel(first_month, premium, charge, mortality, fee_rate, sent, fees, received, scratch, in_sems, out_sems):
    each, count = received.shape[1], fees.shape[0]
    copies = [pltpu.make_async_copy(fee_rate, fees, in_sems.at[0])]
    for i, source in enumerate((premium, charge, mortality)):
        copies.append(pltpu.make_async_copy(source, received.at[i], in_sems.at[i + 1]))
    for copy in copies:
        copy.start()
    for copy in copies:
        copy.wait()
    fee = fees[...]
    grow = jnp.log1p(-fee)
    per_fee = (1.0 - fee) / fee
    for r in range(each):
        for t in range(count):
            at = slice(t * LANES, (t + 1) * LANES)
            row = r * count + t
            scratch[row : row + 1, :] = received[0, r : r + 1, at] - received[1, r : r + 1, at]
            row = (each + r) * count + t
            scratch[row : row + 1, :] = received[2, r : r + 1, at]
    for r in range(each):
        at, then = lines_of(r, count), lines_of(each + r, count)
        month = (first_month[0] + r).astype(jnp.float32)
        scratch[at, :] = scratch[at, :] * (fee * jnp.exp(-(month + 1.0) * grow))
        scratch[then, :] = scratch[then, :] * per_fee
    copies = [pltpu.make_async_copy(scratch, sent.at[i], out_sems.at[i]) for i in range(sent.shape[0])]
    for copy in copies:
        copy.start()
    for copy in copies:
        copy.wait()


def prepare_kernel(lapse_table, lapse_index, fee_rate, level, low, high, lapse):
    fee, index = fee_rate[...], lapse_index[...]
    count = fee.shape[0]
    grow = jnp.log1p(-fee)
    per_fee = (1.0 - fee) / fee
    tables, months = lapse_table.shape

    def one_month(m, carry):
        at = pl.ds(pl.multiple_of(m * count, count), count)
        growth = jnp.exp(-(m.astype(jnp.float32) + 1.0) * grow)
        value = fee * growth
        level[at, :] = value
        low[at, :] = 0.5 * value
        high[at, :] = 1.5 * value
        base = jnp.full(fee.shape, lapse_table[0, m], jnp.float32)
        for k in range(1, tables):
            base = jnp.where(index == k, lapse_table[k, m], base)
        lapse[at, :] = base * (per_fee / growth)
        return carry

    lax.fori_loop(0, months, one_month, 0)


def world_year(start, plan, level, low, high, lapse, cells, state, credit):
    count = cells.shape[1]
    each = plan.shape[1] // (2 * count)
    fee, ratchet, rollup = cells[FEE], cells[RATCHET], cells[ROLLUP]
    kept = 1.0 - fee
    account, surviving, guarantee = state
    per_guarantee = 1.0 / guarantee
    for m in range(start, start + PERIOD):
        d, r = m // each, m % each
        at = lines_of(m, count)
        flow = plan[d, lines_of(r, count), :]
        death = plan[d, lines_of(each + r, count), :]
        account = jnp.maximum(account + flow * per_guarantee, 0.0) * credit(m)
        bounded = jnp.minimum(jnp.maximum(account, low[at, :]), high[at, :])
        surviving = surviving * (kept - fee * death - lapse[at, :] * bounded)
    unit = level[lines_of(start + PERIOD - 1, count), :]
    growth = jnp.maximum(ratchet * (account / unit), 1.0 + rollup_growth * rollup)
    account = jnp.where(ratchet > 0.5, jnp.minimum(account, unit), account / growth)
    return account, surviving, guarantee * growth


def inner_paths(
    start, months, plan, level, low, high, lapse, cells, rows, credit, discount, kept_accounts, kept_growth, reserve
):
    count = cells.shape[1]
    each = plan.shape[1] // (2 * count)
    paths = credit.shape[1]
    groups = paths // SUBLANES
    years = months // PERIOD
    full = (SUBLANES, LANES)

    def tile_step(t, total):
        def spread_out(ref, m):
            return jnp.broadcast_to(ref[pl.ds(m * count + t, 1), :], full)

        def of_cell(ref, r):
            return jnp.broadcast_to(ref[r, pl.ds(t, 1), :], full)

        def planned(m, second):
            d, r = m // each, m % each
            return jnp.broadcast_to(plan[d, pl.ds((r + second * each) * count + t, 1), :], full)

        def group(ref, m, g):
            return ref[m, SUBLANES * g : SUBLANES * (g + 1), :]

        fee = of_cell(cells, FEE)
        kept = 1.0 - fee
        ratchet, rollup = of_cell(cells, RATCHET), of_cell(cells, ROLLUP)
        grown = 1.0 + rollup_growth * rollup
        shrunk = 1.0 / grown
        begin = of_cell(rows, S_ACCOUNT)
        guarantee = of_cell(rows, S_GUARANTEE)
        base = 1.0 / guarantee
        account = [begin] * groups
        per_guarantee = [base] * groups
        for y in range(years):
            for s in range(PERIOD):
                o = y * PERIOD + s
                flow = planned(start + o, 0)
                if y == 0:
                    flow = flow * base
                for g in range(groups):
                    term = flow if y == 0 else flow * per_guarantee[g]
                    account[g] = jnp.maximum(account[g] + term, 0.0) * group(credit, o, g)
                    kept_accounts[o, SUBLANES * g : SUBLANES * (g + 1), :] = account[g]
            if y + 1 < years:
                unit = spread_out(level, start + y * PERIOD + PERIOD - 1)
                per_unit = ratchet / unit
                cap = jnp.where(ratchet > 0.5, unit, 1e30)
                for g in range(groups):
                    growth = jnp.maximum(per_unit * account[g], grown)
                    kept_growth[y, SUBLANES * g : SUBLANES * (g + 1), :] = growth
                    per_guarantee[g] = per_guarantee[g] / growth
                    account[g] = jnp.minimum(account[g], cap) * shrunk
                    kept_growth[years + y, SUBLANES * g : SUBLANES * (g + 1), :] = account[g]
        worth = [None] * groups
        for o in reversed(range(months)):
            m = start + o
            unit, least, most = spread_out(level, m), spread_out(low, m), spread_out(high, m)
            lapsing = spread_out(lapse, m)
            death = planned(m, 1)
            staying = kept - fee * death
            for g in range(groups):
                after = group(kept_accounts, o, g)
                if o == 0:
                    before = begin
                elif o % PERIOD == 0:
                    before = group(kept_growth, years + o // PERIOD - 1, g)
                else:
                    before = group(kept_accounts, o - 1, g)
                value = death * jnp.maximum(unit - after, 0.0) - before
                if worth[g] is not None:
                    later = worth[g]
                    if (o + 1) % PERIOD == 0:
                        later = later * group(kept_growth, o // PERIOD, g)
                    bounded = jnp.minimum(jnp.maximum(after, least), most)
                    value = value + (staying - lapsing * bounded) * later
                worth[g] = value * group(discount, o, g)
        summed = worth[0]
        for g in range(1, groups):
            summed = summed + worth[g]
        scale = guarantee * of_cell(rows, S_SURVIVING) * (1.0 / paths)
        row = jnp.sum(summed * scale, axis=0, keepdims=True)
        reserve[0:1, pl.ds(pl.multiple_of(t * LANES, LANES), LANES)] = row
        return total + row

    return lax.fori_loop(0, count, tile_step, jnp.zeros((1, LANES), jnp.float32))


def fill_tables(first, months, spread, sources, credit, discount):
    for part, source in enumerate(sources):
        rates = source[...]
        lines = rates.shape[0]
        crediting = 1.0 + jnp.maximum(rates - spread, credit_floor)
        discounting = jnp.exp(-rates)
        for m in range(months):
            at = slice(part * lines, (part + 1) * lines)
            credit[m, at, :] = jnp.broadcast_to(crediting[:, first + m : first + m + 1], (lines, LANES))
            discount[m, at, :] = jnp.broadcast_to(discounting[:, first + m : first + m + 1], (lines, LANES))


def block_sums(value, parts, block_hot):
    parts[...] = jnp.zeros_like(parts)
    for part in range(3):
        rounded = value.astype(jnp.bfloat16).astype(jnp.float32)
        parts[part : part + 1, :] = rounded
        value = value - rounded
    sums = jnp.dot(parts[...].astype(jnp.bfloat16), block_hot[...], preferred_element_type=jnp.float32)
    return sums[0:1, :] + sums[1:2, :] + sums[2:3, :]


def first_kernel(
    owners, months, cell_at, world, spread, plan, level, low, high, lapse, cells, own, near, far, across, block_hot,
    reserve, rows, kept_here, next_one, next_two, next_three, credit, discount, kept_accounts, kept_growth, parts, shares,
):
    fill_tables(0, months, spread[0], (own, near, far, across), credit, discount)
    fee, guarantee = cells[FEE], cells[GUARANTEE]
    account = fee * cells[ACCOUNT] / guarantee
    state = (account, jnp.ones_like(account), guarantee)
    state = world_year(
        0, plan, level, low, high, lapse, cells, state, lambda m: 1.0 + jnp.maximum(world[m] - spread[0], credit_floor)
    )
    for r, value in enumerate(state):
        rows[r] = value
    total = inner_paths(
        PERIOD, months, plan, level, low, high, lapse, cells, rows, credit, discount, kept_accounts, kept_growth, reserve
    )
    half = LANES // 2
    sums = block_sums(reserve[...], parts, block_hot)
    total = jnp.broadcast_to(jnp.sum(total, axis=1, keepdims=True), (1, half))
    for k in range(owners):
        shares[k : k + 1, :] = jnp.concatenate([sums[:, half * k : half * (k + 1)], total], axis=1)
    for s, target in enumerate((kept_here, next_one, next_two, next_three)):
        target[...] = shares[pl.ds(lax.rem(cell_at[0] + s, owners), 1), :]


def second_kernel(
    cells_all, months, world, spread, place, kept_here, next_one, next_two, next_three,
    plan, level, low, high, lapse, cells, own, near, far, across, rows_one, reserve_one, block_hot,
    reserves, parcel, blocks_one, rows, reserve, credit, discount, kept_accounts, kept_growth, parts,
):
    half = LANES // 2
    whole = kept_here[...] + next_one[...] + next_two[...] + next_three[...]
    blocks_one[...] = whole
    spread_two = (spread[0] * (1.0 + jnp.tanh(whole / cells_all)))[0, half]
    fill_tables(own.shape[1] - months, months, spread_two, (own, near, far, across), credit, discount)
    state = tuple(rows_one[r] for r in range(3))
    state = world_year(
        PERIOD, plan, level, low, high, lapse, cells, state,
        lambda m: 1.0 + jnp.maximum(world[m] - spread_two, credit_floor),
    )
    for r, value in enumerate(state):
        rows[r] = value
    total = inner_paths(
        2 * PERIOD, months, plan, level, low, high, lapse, cells, rows, credit, discount, kept_accounts, kept_growth, reserve
    )
    reserves[0] = reserve_one[...]
    reserves[1] = reserve[...]
    sums = block_sums(reserve[...], parts, block_hot)
    rate_sum = world[PERIOD]
    for m in range(PERIOD + 1, 2 * PERIOD):
        rate_sum = rate_sum + world[m]
    discount_world = jnp.exp(jnp.full((1, LANES), -rate_sum, jnp.float32))
    total_two = jnp.broadcast_to(jnp.sum(total, axis=1, keepdims=True), (1, LANES))
    loss = (discount_world * total_two - kept_here[...]) / cells_all
    lane = lax.broadcasted_iota(jnp.int32, (1, LANES), 1)
    loss = jnp.where(lane == half + place[0], loss, 0.0)
    for k in range(parcel.shape[1]):
        line = jnp.concatenate([sums[:, half * k : half * (k + 1)], loss[:, half:]], axis=1)
        parcel[:, k] = jnp.broadcast_to(line[None], (parcel.shape[0], 1, LANES))


def last_kernel(place, received, blocks_one, block_reserve, capital):
    outers, owners = received.shape[0], received.shape[1]
    half = LANES // 2
    losses = received[:, 0, 0, :]
    for k in range(1, owners):
        losses = losses + received[:, k, 0, :]
    lane = lax.broadcasted_iota(jnp.int32, losses.shape, 1) - half
    losses = jnp.where(lane >= 0, losses, 0.0)
    across = jnp.sum(losses, axis=0, keepdims=True)
    down = jnp.sum(losses, axis=1, keepdims=True)
    place_down = lax.broadcasted_iota(jnp.int32, losses.shape, 0)
    ahead = (across > down) | ((across == down) & (lane < place_down))
    ahead = ahead & (lane >= 0)
    rank = jnp.sum(jnp.where(ahead, 1.0, 0.0), axis=1, keepdims=True)
    count_top = outers // 4
    chosen = jnp.where(rank < count_top - 0.5, down, 0.0)
    capital[...] = jnp.broadcast_to(jnp.sum(chosen, axis=0, keepdims=True) / count_top, capital.shape)
    blocks = received[place[0], 0]
    for k in range(1, owners):
        blocks = blocks + received[place[0], k]
    block_reserve[0] = blocks_one[:, :half]
    block_reserve[1] = blocks[:, :half]


VMEM = pl.BlockSpec(memory_space=pltpu.VMEM)
SMEM = pl.BlockSpec(memory_space=pltpu.SMEM)
HBM = pl.BlockSpec(memory_space=pltpu.HBM)
MEBI = 1024 * 1024


def body(
    premium,
    charge,
    mortality,
    lapse_table,
    lapse_index,
    guarantee_type,
    block_index,
    account_start,
    guarantee_start,
    fee_rate,
    first_rates,
    second_rates,
    world_rates,
    spread,
):
    f32 = jnp.float32
    outer_size, inner_size, cell_size = (lax.axis_size(a) for a in ALL)
    each, local = premium.shape
    months_all = each * outer_size
    inner_at = lax.axis_index("inner")
    place = lax.axis_index("outer") * inner_size + inner_at
    paths = first_rates.shape[1] * inner_size
    months_one, months_two = first_rates.shape[2], second_rates.shape[2]
    cells_all = local * cell_size
    block_count = 4 * cells_all // LANES

    count = local // LANES
    fee = fee_rate.reshape(count, LANES)

    def call(kernel, name, outs, specs, scratch=(), out_space=VMEM, limit=16):
        return pl.pallas_call(
            kernel,
            out_shape=outs,
            in_specs=specs,
            out_specs=jax.tree.map(lambda _: out_space, outs),
            scratch_shapes=list(scratch),
            compiler_params=pltpu.CompilerParams(vmem_limit_bytes=limit * MEBI),
            name=name,
        )

    def floats(*lengths):
        return jax.ShapeDtypeStruct(lengths, f32)

    def held(*lengths):
        return pltpu.VMEM(lengths, f32)

    first_month = (lax.axis_index("outer") * each).astype(jnp.int32).reshape(1)
    sent = call(
        parcel_kernel,
        "parcel",
        floats(outer_size, 2 * each * count, LANES),
        [SMEM] + [HBM] * 4,
        [
            held(count, LANES),
            held(3, each, local),
            held(2 * each * count, LANES),
            pltpu.SemaphoreType.DMA((4,)),
            pltpu.SemaphoreType.DMA((outer_size,)),
        ],
        HBM,
        60,
    )(first_month, premium, charge, mortality, fee)
    sent, first_rates, second_rates = lax.optimization_barrier((sent, first_rates, second_rates))
    rates = jnp.concatenate([first_rates, second_rates], axis=2)
    plan = lax.all_to_all(sent, "outer", 0, 0, tiled=True)
    shares = [
        lax.dynamic_index_in_dim(rates, jnp.bitwise_xor(inner_at, s), 0, False) for s in range(inner_size)
    ]
    shares[1:] = [
        lax.ppermute(shares[s], "inner", [(j, j ^ s) for j in range(inner_size)]) for s in range(1, inner_size)
    ]
    shaped = [floats(months_all * count, LANES)] * 4
    level, low, high, lapse = call(prepare_kernel, "prepare", shaped, [SMEM] + [VMEM] * 2)(
        lapse_table, lapse_index.reshape(count, LANES), fee
    )
    cells = jnp.stack(
        [
            fee_rate,
            account_start,
            guarantee_start,
            (guarantee_type == 1).astype(f32),
            (guarantee_type == 2).astype(f32),
        ]
    ).reshape(-1, count, LANES)
    world = lax.dynamic_index_in_dim(world_rates, inner_at, 0, False)
    spread_own = lax.dynamic_slice_in_dim(spread, inner_at, 1, 0)
    cell_at = lax.axis_index("cell").astype(jnp.int32).reshape(1)
    place_own = place.astype(jnp.int32).reshape(1)
    block_hot = (block_index[:, None] == jnp.arange(block_count)[None, :]).astype(jnp.bfloat16)

    def inner_scratch(months):
        years = months // PERIOD
        return [
            held(months, paths, LANES),
            held(months, paths, LANES),
            held(months, paths, LANES),
            held(2 * years, paths, LANES),
        ]

    line = floats(1, LANES)
    state = floats(3, count, LANES)
    reserve_one, rows_one, kept_here, *others = call(
        functools.partial(first_kernel, cell_size, months_one),
        "first_date",
        [floats(1, local), state, line, line, line, line],
        [SMEM] * 3 + [VMEM] * 11,
        inner_scratch(months_one) + [held(SUBLANES, local), held(cell_size, LANES)],
    )(cell_at, world, spread_own, plan, level, low, high, lapse, cells, *shares, block_hot)

    others = [
        lax.ppermute(others[s - 1], "cell", [(k, (k + s) % cell_size) for k in range(cell_size)])
        for s in range(1, cell_size)
    ]

    reserves, parcel, blocks_one = call(
        functools.partial(second_kernel, cells_all, months_two),
        "second_date",
        [floats(2, 1, local), floats(outer_size * inner_size, cell_size, 1, LANES), line],
        [SMEM] * 3 + [VMEM] * 17,
        [held(3, count, LANES), held(1, local)] + inner_scratch(months_two) + [held(SUBLANES, local)],
    )(
        world, spread_own, place_own, kept_here, *others,
        plan, level, low, high, lapse, cells, *shares, rows_one, reserve_one, block_hot,
    )

    received = lax.all_to_all(parcel.reshape(-1, 1, LANES), ALL, 0, 0, tiled=True)
    block_reserve, capital = call(
        last_kernel, "last_sums", [floats(2, 1, block_count // cell_size), line], [SMEM] + [VMEM] * 2
    )(place_own, received.reshape(parcel.shape), blocks_one)
    return reserves, block_reserve, capital[0, :1]


def solution(mesh):
    placed = (
        P("outer", "cell"),
        P("outer", "cell"),
        P("outer", "cell"),
        P(),
        P("cell"),
        P("cell"),
        P("cell"),
        P("cell"),
        P("cell"),
        P("cell"),
        P("outer", "inner", None),
        P("outer", "inner", None),
        P("outer", None),
        P("outer"),
    )
    return jax.shard_map(
        body,
        mesh=mesh,
        in_specs=placed,
        out_specs=(P(None, ("outer", "inner"), "cell"), P(None, ("outer", "inner"), "cell"), P()),
        check_vma=False,
    )
```

```python
import functools

import jax
import jax.numpy as jnp
from jax import lax
from jax.experimental import pallas as pl
from jax.experimental.pallas import tpu as pltpu
from jax.sharding import PartitionSpec as P

PERIOD = 12
LANES = 128
SUBLANES = 8
TOGETHER = 2
CORES = 2

credit_floor = 0.001
rollup_growth = 0.05
ALL = ("outer", "inner", "cell")

FEE, ACCOUNT, GUARANTEE, RATCHET, ROLLUP = range(5)
S_ACCOUNT, S_SURVIVING, S_GUARANTEE = range(3)


def lines_of(month, count):
    return slice(month * count, (month + 1) * count)


def parcel_kernel(outer_at, inner_at, premium, charge, mortality, fee_rate, sent, fees, received, scratch, in_sems, out_sems):
    each, wide = received.shape[1:]
    count = fees.shape[0]
    half = lax.rem(inner_at[0], CORES)
    copies = [pltpu.make_async_copy(fee_rate.at[half], fees, in_sems.at[0])]
    columns = pl.ds(pl.multiple_of(half * wide, wide), wide)
    for i, source in enumerate((premium, charge, mortality)):
        copies.append(pltpu.make_async_copy(source.at[:, columns], received.at[i], in_sems.at[i + 1]))
    for copy in copies:
        copy.start()
    for copy in copies:
        copy.wait()
    fee = fees[...]
    grow = jnp.log1p(-fee)
    per_fee = (1.0 - fee) / fee
    for r in range(each):
        for t in range(count):
            at = slice(t * LANES, (t + 1) * LANES)
            row = r * count + t
            scratch[row : row + 1, :] = received[0, r : r + 1, at] - received[1, r : r + 1, at]
            row = (each + r) * count + t
            scratch[row : row + 1, :] = received[2, r : r + 1, at]
    for r in range(each):
        at, then = lines_of(r, count), lines_of(each + r, count)
        month = (outer_at[0] * each + r).astype(jnp.float32)
        scratch[at, :] = scratch[at, :] * (fee * jnp.exp(-(month + 1.0) * grow))
        scratch[then, :] = scratch[then, :] * per_fee
    copies = [pltpu.make_async_copy(scratch, sent.at[i], out_sems.at[i]) for i in range(sent.shape[0])]
    for copy in copies:
        copy.start()
    for copy in copies:
        copy.wait()


def prepare_kernel(
    inner_at, lapse_table, lapse_index, kind, account, guarantee, fee_rate, cells, level, low, high, lapse, indices
):
    half = lax.rem(inner_at[0], CORES)
    for part, source in enumerate((half, 1 - half)):
        at = lines_of(part, kind.shape[1])
        cells[FEE, at, :] = fee_rate[source]
        cells[ACCOUNT, at, :] = account[source]
        cells[GUARANTEE, at, :] = guarantee[source]
        cells[RATCHET, at, :] = jnp.where(kind[source] == 1, 1.0, 0.0)
        cells[ROLLUP, at, :] = jnp.where(kind[source] == 2, 1.0, 0.0)
        indices[at, :] = lapse_index[source]
    fee, index = cells[FEE], indices[...]
    count = fee.shape[0]
    grow = jnp.log1p(-fee)
    per_fee = (1.0 - fee) / fee
    tables, months = lapse_table.shape

    def one_month(m, carry):
        at = pl.ds(pl.multiple_of(m * count, count), count)
        growth = jnp.exp(-(m.astype(jnp.float32) + 1.0) * grow)
        value = fee * growth
        level[at, :] = value
        low[at, :] = 0.5 * value
        high[at, :] = 1.5 * value
        base = jnp.full(fee.shape, lapse_table[0, m], jnp.float32)
        for k in range(1, tables):
            base = jnp.where(index == k, lapse_table[k, m], base)
        lapse[at, :] = base * (per_fee / growth)
        return carry

    lax.fori_loop(0, months, one_month, 0)


def fill_first_tables(inner_at, spread, own, near, far, across, credit, discount):
    lines = own.shape[0]
    for part, rates in enumerate((own[...], near[...], far[:lines, :], across[lines:, :])):
        at = slice(part * lines, (part + 1) * lines)
        crediting = 1.0 + jnp.maximum(rates - spread[inner_at[0]], credit_floor)
        discounting = jnp.exp(-rates)
        for m in range(credit.shape[0]):
            credit[m, at, :] = jnp.broadcast_to(crediting[:, m : m + 1], (lines, LANES))
            discount[m, at, :] = jnp.broadcast_to(discounting[:, m : m + 1], (lines, LANES))


def second_table_kernel(own, near, far, across, rate, discount):
    first = own.shape[1] - rate.shape[0]
    lines = own.shape[0]
    for part, rates in enumerate((own[...], near[...], far[:lines, :], across[lines:, :])):
        at = slice(part * lines, (part + 1) * lines)
        discounting = jnp.exp(-rates)
        for m in range(rate.shape[0]):
            rate[m, at, :] = jnp.broadcast_to(rates[:, first + m : first + m + 1], (lines, LANES))
            discount[m, at, :] = jnp.broadcast_to(discounting[:, first + m : first + m + 1], (lines, LANES))


def world_year(start, part, plan, level, low, high, lapse, cells, state, credit):
    count = cells.shape[1]
    own = count // CORES
    each = plan.shape[1] // (2 * own)
    here = lines_of(part, own)
    fee, ratchet, rollup = cells[FEE, here, :], cells[RATCHET, here, :], cells[ROLLUP, here, :]
    kept = 1.0 - fee
    account, surviving, guarantee = state
    per_guarantee = 1.0 / guarantee
    for m in range(start, start + PERIOD):
        d, r = m // each, m % each
        at = slice(m * count + part * own, m * count + (part + 1) * own)
        flow = plan[d, lines_of(r, own), :]
        death = plan[d, lines_of(each + r, own), :]
        account = jnp.maximum(account + flow * per_guarantee, 0.0) * credit(m)
        bounded = jnp.minimum(jnp.maximum(account, low[at, :]), high[at, :])
        surviving = surviving * (kept - fee * death - lapse[at, :] * bounded)
        unit = level[at, :]
    growth = jnp.maximum(ratchet * (account / unit), 1.0 + rollup_growth * rollup)
    account = jnp.where(ratchet > 0.5, jnp.minimum(account, unit), account / growth)
    return account, surviving, guarantee * growth


def inner_paths(
    start, part, target, plan, level, low, high, lapse, cells, rows, credit, discount, kept_accounts, kept_growth, reserve
):
    count = cells.shape[1]
    own = count // CORES
    each = plan.shape[1] // (2 * own)
    months, paths = credit.shape[:2]
    groups = paths // SUBLANES
    years = months // PERIOD
    full = (SUBLANES, LANES)

    def group(ref, m, g):
        return ref[m, SUBLANES * g : SUBLANES * (g + 1), :]

    def tiles_step(step, total):
        def spread_out(ref, i, m):
            return jnp.broadcast_to(ref[pl.ds(m * count + part * own + step * TOGETHER + i, 1), :], full)

        def of_cell(i, r):
            return jnp.broadcast_to(cells[r, pl.ds(part * own + step * TOGETHER + i, 1), :], full)

        def of_state(i, r):
            return jnp.broadcast_to(rows[r, pl.ds(step * TOGETHER + i, 1), :], full)

        def planned(i, m, second):
            d, r = m // each, m % each
            return jnp.broadcast_to(plan[d, pl.ds((r + second * each) * own + step * TOGETHER + i, 1), :], full)

        def of_tile(ref, i, m, g):
            return ref[i, m, SUBLANES * g : SUBLANES * (g + 1), :]

        def keep(ref, i, m, g, value):
            ref[i, m, SUBLANES * g : SUBLANES * (g + 1), :] = value

        tiles = range(TOGETHER)
        begin = [of_state(i, S_ACCOUNT) for i in tiles]
        base = [1.0 / of_state(i, S_GUARANTEE) for i in tiles]
        account = [[begin[i]] * groups for i in tiles]
        per_guarantee = [[base[i]] * groups for i in tiles]
        for o in range(months):
            flow = [planned(i, start + o, 0) for i in tiles]
            if o < PERIOD:
                flow = [flow[i] * base[i] for i in tiles]
            for g in range(groups):
                crediting = group(credit, o, g)
                for i in tiles:
                    term = flow[i] if o < PERIOD else flow[i] * per_guarantee[i][g]
                    account[i][g] = jnp.maximum(account[i][g] + term, 0.0) * crediting
                    keep(kept_accounts, i, o, g, account[i][g])
            if (o + 1) % PERIOD == 0 and o + 1 < months:
                y = o // PERIOD
                for i in tiles:
                    ratchet = of_cell(i, RATCHET)
                    grown = 1.0 + rollup_growth * of_cell(i, ROLLUP)
                    shrunk = 1.0 / grown
                    unit = spread_out(level, i, start + o)
                    per_unit = ratchet / unit
                    cap = jnp.where(ratchet > 0.5, unit, 1e30)
                    for g in range(groups):
                        growth = jnp.maximum(per_unit * account[i][g], grown)
                        keep(kept_growth, i, y, g, growth)
                        per_guarantee[i][g] = per_guarantee[i][g] / growth
                        account[i][g] = jnp.minimum(account[i][g], cap) * shrunk
                        keep(kept_growth, i, years + y, g, account[i][g])
        fee = [of_cell(i, FEE) for i in tiles]
        worth = [[None] * groups for i in tiles]
        for o in reversed(range(months)):
            m = start + o
            for i in tiles:
                unit, least, most = spread_out(level, i, m), spread_out(low, i, m), spread_out(high, i, m)
                lapsing = spread_out(lapse, i, m)
                death = planned(i, m, 1)
                staying = (1.0 - fee[i]) - fee[i] * death
                for g in range(groups):
                    after = of_tile(kept_accounts, i, o, g)
                    if o == 0:
                        before = begin[i]
                    elif o % PERIOD == 0:
                        before = of_tile(kept_growth, i, years + o // PERIOD - 1, g)
                    else:
                        before = of_tile(kept_accounts, i, o - 1, g)
                    value = death * jnp.maximum(unit - after, 0.0) - before
                    if worth[i][g] is not None:
                        later = worth[i][g]
                        if (o + 1) % PERIOD == 0:
                            later = later * of_tile(kept_growth, i, o // PERIOD, g)
                        bounded = jnp.minimum(jnp.maximum(after, least), most)
                        value = value + (staying - lapsing * bounded) * later
                    worth[i][g] = value * group(discount, o, g)
        for i in tiles:
            summed = worth[i][0]
            for g in range(1, groups):
                summed = summed + worth[i][g]
            scale = of_state(i, S_GUARANTEE) * of_state(i, S_SURVIVING) * (1.0 / paths)
            row = jnp.sum(summed * scale, axis=0, keepdims=True)
            at = pl.multiple_of((target + step * TOGETHER + i) * LANES, LANES)
            reserve[0:1, pl.ds(at, LANES)] = row
            total = total + row
        return total

    return lax.fori_loop(0, own // TOGETHER, tiles_step, jnp.zeros((1, LANES), jnp.float32))


def block_sums(value, parts, block_hot):
    parts[...] = jnp.zeros_like(parts)
    for part in range(3):
        rounded = value.astype(jnp.bfloat16).astype(jnp.float32)
        parts[part : part + 1, :] = rounded
        value = value - rounded
    sums = jnp.dot(parts[...].astype(jnp.bfloat16), block_hot[...], preferred_element_type=jnp.float32)
    return sums[0:1, :] + sums[1:2, :] + sums[2:3, :]


def first_half(part, inner_at, world, spread, plan, level, low, high, lapse, cells, credit, discount, reserve, rows, kept_accounts, kept_growth):
    own = cells.shape[1] // CORES
    at, here = inner_at[0], lines_of(part, own)
    half = lax.rem(at, CORES)
    fee, guarantee = cells[FEE, here, :], cells[GUARANTEE, here, :]
    account = fee * cells[ACCOUNT, here, :] / guarantee
    state = (account, jnp.ones_like(account), guarantee)
    state = world_year(
        0, part, plan, level, low, high, lapse, cells, state,
        lambda m: 1.0 + jnp.maximum(world[at, m] - spread[at], credit_floor),
    )
    for r, value in enumerate(state):
        rows[r] = value
    target = (half if part == 0 else 1 - half) * own
    return inner_paths(
        PERIOD, part, target, plan, level, low, high, lapse, cells, rows, credit, discount, kept_accounts, kept_growth, reserve
    )


def first_own_kernel(
    inner_at, world, spread, plan, level, low, high, lapse, cells, own_rates, near_rates, far_rates, across_rates,
    reserve, rows, total, credit, discount, kept_accounts, kept_growth,
):
    fill_first_tables(inner_at, spread, own_rates, near_rates, far_rates, across_rates, credit, discount)
    total[...] = first_half(
        0, inner_at, world, spread, plan, level, low, high, lapse, cells, credit, discount, reserve, rows, kept_accounts, kept_growth
    )


def first_other_kernel(
    owners, inner_at, cell_at, world, spread, plan, level, low, high, lapse, cells, credit, discount,
    reserve_own, total_own, block_hot,
    reserve, rows, kept_here, next_one, next_two, next_three, kept_accounts, kept_growth, parts, shares,
):
    reserve[...] = reserve_own[...]
    total = total_own[...] + first_half(
        1, inner_at, world, spread, plan, level, low, high, lapse, cells, credit, discount, reserve, rows, kept_accounts, kept_growth
    )
    half = LANES // 2
    sums = block_sums(reserve[...], parts, block_hot)
    total = jnp.broadcast_to(jnp.sum(total, axis=1, keepdims=True), (1, half))
    for k in range(owners):
        shares[k : k + 1, :] = jnp.concatenate([sums[:, half * k : half * (k + 1)], total], axis=1)
    for s, target in enumerate((kept_here, next_one, next_two, next_three)):
        target[...] = shares[pl.ds(lax.rem(cell_at[0] + s, owners), 1), :]


def second_kernel(
    cells_all, inner_at, world, spread, place, kept_here, next_one, next_two, next_three,
    plan_own, plan_other, level, low, high, lapse, cells, rate, discount, rows_own, rows_other, reserve_one, block_hot,
    reserves, parcel, blocks_one, rows, reserve, credit, kept_accounts, kept_growth, parts,
):
    half = LANES // 2
    at = inner_at[0]
    own = cells.shape[1] // CORES
    whole = kept_here[...] + next_one[...] + next_two[...] + next_three[...]
    blocks_one[...] = whole
    spread_two = (spread[at] * (1.0 + jnp.tanh(whole / cells_all)))[0, half]
    for m in range(credit.shape[0]):
        credit[m] = 1.0 + jnp.maximum(rate[m] - spread_two, credit_floor)
    core = lax.rem(at, CORES)
    total = jnp.zeros((1, LANES), jnp.float32)
    for part, (plan, source) in enumerate(((plan_own, rows_own), (plan_other, rows_other))):
        state = world_year(
            PERIOD, part, plan, level, low, high, lapse, cells, tuple(source[r] for r in range(3)),
            lambda m: 1.0 + jnp.maximum(world[at, m] - spread_two, credit_floor),
        )
        for r, value in enumerate(state):
            rows[part, r] = value
    for part, plan in enumerate((plan_own, plan_other)):
        total = total + inner_paths(
            2 * PERIOD, part, (core if part == 0 else 1 - core) * own,
            plan, level, low, high, lapse, cells, rows.at[part], credit, discount, kept_accounts, kept_growth, reserve,
        )
    reserves[0] = reserve_one[...]
    reserves[1] = reserve[...]
    sums = block_sums(reserve[...], parts, block_hot)
    rate_sum = world[at, PERIOD]
    for m in range(PERIOD + 1, 2 * PERIOD):
        rate_sum = rate_sum + world[at, m]
    discount_world = jnp.exp(jnp.full((1, LANES), -rate_sum, jnp.float32))
    total_two = jnp.broadcast_to(jnp.sum(total, axis=1, keepdims=True), (1, LANES))
    loss = (discount_world * total_two - kept_here[...]) / cells_all
    lane = lax.broadcasted_iota(jnp.int32, (1, LANES), 1)
    loss = jnp.where(lane == half + place[0], loss, 0.0)
    for k in range(parcel.shape[1]):
        line = jnp.concatenate([sums[:, half * k : half * (k + 1)], loss[:, half:]], axis=1)
        parcel[:, k] = jnp.broadcast_to(line[None], (parcel.shape[0], 1, LANES))


def last_kernel(place, received, blocks_one, block_reserve, capital):
    outers, owners = received.shape[0], received.shape[1]
    half = LANES // 2
    losses = received[:, 0, 0, :]
    for k in range(1, owners):
        losses = losses + received[:, k, 0, :]
    lane = lax.broadcasted_iota(jnp.int32, losses.shape, 1) - half
    losses = jnp.where(lane >= 0, losses, 0.0)
    across = jnp.sum(losses, axis=0, keepdims=True)
    down = jnp.sum(losses, axis=1, keepdims=True)
    place_down = lax.broadcasted_iota(jnp.int32, losses.shape, 0)
    ahead = (across > down) | ((across == down) & (lane < place_down))
    ahead = ahead & (lane >= 0)
    rank = jnp.sum(jnp.where(ahead, 1.0, 0.0), axis=1, keepdims=True)
    count_top = outers // 4
    chosen = jnp.where(rank < count_top - 0.5, down, 0.0)
    capital[...] = jnp.broadcast_to(jnp.sum(chosen, axis=0, keepdims=True) / count_top, capital.shape)
    blocks = received[place[0], 0]
    for k in range(1, owners):
        blocks = blocks + received[place[0], k]
    block_reserve[0] = blocks_one[:, :half]
    block_reserve[1] = blocks[:, :half]


VMEM = pl.BlockSpec(memory_space=pltpu.VMEM)
SMEM = pl.BlockSpec(memory_space=pltpu.SMEM)
HBM = pl.BlockSpec(memory_space=pltpu.HBM)
MEBI = 1024 * 1024


def call(kernel, name, outs, specs, scratch=(), out_space=VMEM, limit=16, read=0):
    return pl.pallas_call(
        kernel,
        out_shape=outs,
        in_specs=specs,
        out_specs=jax.tree.map(lambda _: out_space, outs),
        scratch_shapes=list(scratch),
        compiler_params=pltpu.CompilerParams(vmem_limit_bytes=limit * MEBI),
        name=name,
        cost_estimate=pl.CostEstimate(flops=4000 * read, bytes_accessed=read, transcendentals=0),
    )


def floats(*lengths):
    return jax.ShapeDtypeStruct(lengths, jnp.float32)


def held(*lengths):
    return pltpu.VMEM(lengths, jnp.float32)


def body(
    premium,
    charge,
    mortality,
    lapse_table,
    lapse_index,
    guarantee_type,
    block_index,
    account_start,
    guarantee_start,
    fee_rate,
    first_rates,
    second_rates,
    world_rates,
    spread,
):
    outer_size, inner_size, cell_size = (lax.axis_size(a) for a in ALL)
    each, local = premium.shape
    months_all = each * outer_size
    paths = first_rates.shape[1] * inner_size
    months_one, months_two = first_rates.shape[2], second_rates.shape[2]
    cells_all = local * cell_size
    block_count = 4 * cells_all // LANES
    count = local // LANES
    own = count // CORES

    outer_at, inner_at, cell_at = (lax.axis_index(a).astype(jnp.int32) for a in ALL)
    place = (outer_at * inner_size + inner_at).reshape(1)
    outer_at, inner_one, cell_at = outer_at.reshape(1), inner_at.reshape(1), cell_at.reshape(1)

    def halves(value):
        return value.reshape(CORES, own, LANES)

    sent = call(
        parcel_kernel,
        "parcel",
        floats(outer_size, 2 * each * own, LANES),
        [SMEM] * 2 + [HBM] * 4,
        [
            held(own, LANES),
            held(3, each, own * LANES),
            held(2 * each * own, LANES),
            pltpu.SemaphoreType.DMA((4,)),
            pltpu.SemaphoreType.DMA((outer_size,)),
        ],
        HBM,
        60,
    )(outer_at, inner_one, premium, charge, mortality, halves(fee_rate))
    sent, first_rates, second_rates = lax.optimization_barrier((sent, first_rates, second_rates))
    rates = jnp.concatenate([first_rates, second_rates], axis=2)
    plan_own = lax.all_to_all(sent, "outer", 0, 0, tiled=True)
    own_rates, near_rates, far_rates, across_rates = (
        lax.dynamic_index_in_dim(rates, jnp.bitwise_xor(inner_at, s), 0, False) for s in range(inner_size)
    )
    far_rates = jnp.concatenate([far_rates, across_rates], axis=0)

    def swapped(value, s):
        return lax.ppermute(value, "inner", [(j, j ^ s) for j in range(inner_size)])

    far_rates = swapped(far_rates, CORES)
    near_rates = swapped(near_rates, 1)
    across_rates = swapped(far_rates, 1)
    shares = [own_rates, near_rates, far_rates, across_rates]
    coefs = [floats(5, count, LANES)] + [floats(months_all * count, LANES)] * 4
    cells, *coefs = call(prepare_kernel, "prepare", coefs, [SMEM] * 2 + [VMEM] * 5, [pltpu.VMEM((count, LANES), jnp.int32)], read=4 * MEBI)(
        inner_one,
        lapse_table,
        *(halves(a) for a in (lapse_index, guarantee_type, account_start, guarantee_start, fee_rate)),
    )
    block_hot = (block_index[:, None] == jnp.arange(block_count)[None, :]).astype(jnp.bfloat16)

    plan_other = swapped(plan_own, 1)

    def inner_scratch(months):
        return [
            held(TOGETHER, months, paths, LANES),
            held(TOGETHER, 2 * (months // PERIOD), paths, LANES),
        ]

    line = floats(1, LANES)
    state = floats(3, own, LANES)
    table = floats(months_one, paths, LANES)
    reserve_own, rows_own, total_own, credit_one, discount_one = call(
        first_own_kernel,
        "first_date_own",
        [floats(1, local), state, line, table, table],
        [SMEM] * 3 + [VMEM] * 10,
        inner_scratch(months_one),
        read=20 * MEBI,
    )(inner_one, world_rates, spread, plan_own, *coefs, cells, *shares)
    reserve_one, rows_other, kept_here, *others = call(
        functools.partial(first_other_kernel, cell_size),
        "first_date_other",
        [floats(1, local), state, line, line, line, line],
        [SMEM] * 4 + [VMEM] * 11,
        inner_scratch(months_one) + [held(SUBLANES, local), held(cell_size, LANES)],
    )(
        inner_one, cell_at, world_rates, spread, plan_other, *coefs, cells, credit_one, discount_one,
        reserve_own, total_own, block_hot,
    )

    others = [
        lax.ppermute(others[s - 1], "cell", [(k, (k + s) % cell_size) for k in range(cell_size)])
        for s in range(1, cell_size)
    ]
    reserve_one, *shares = lax.optimization_barrier((reserve_one, *shares))
    rate_two, discount_two = call(
        second_table_kernel, "second_tables", [floats(months_two, paths, LANES)] * 2, [VMEM] * 4
    )(*shares)

    reserves, parcel, blocks_one = call(
        functools.partial(second_kernel, cells_all),
        "second_date",
        [floats(2, 1, local), floats(outer_size * inner_size, cell_size, 1, LANES), line],
        [SMEM] * 4 + [VMEM] * 17,
        [held(CORES, 3, own, LANES), held(1, local), held(months_two, paths, LANES)]
        + inner_scratch(months_two)
        + [held(SUBLANES, local)],
    )(
        inner_one, world_rates, spread, place, kept_here, *others,
        plan_own, plan_other, *coefs, cells, rate_two, discount_two, rows_own, rows_other, reserve_one, block_hot,
    )

    received = lax.all_to_all(parcel.reshape(-1, 1, LANES), ALL, 0, 0, tiled=True)
    block_reserve, capital = call(
        last_kernel, "last_sums", [floats(2, 1, block_count // cell_size), line], [SMEM] + [VMEM] * 2
    )(place, received.reshape(parcel.shape), blocks_one)
    return reserves, block_reserve, capital[0, :1]


def solution(mesh):
    placed = (
        P("outer", "cell"),
        P("outer", "cell"),
        P("outer", "cell"),
        P(),
        P("cell"),
        P("cell"),
        P("cell"),
        P("cell"),
        P("cell"),
        P("cell"),
        P("outer", "inner", None),
        P("outer", "inner", None),
        P("outer", None),
        P("outer"),
    )
    return jax.shard_map(
        body,
        mesh=mesh,
        in_specs=placed,
        out_specs=(P(None, ("outer", "inner"), "cell"), P(None, ("outer", "inner"), "cell"), P()),
        check_vma=False,
    )
```

```python
import functools

import jax
import jax.numpy as jnp
from jax import lax
from jax.experimental import pallas as pl
from jax.experimental.pallas import tpu as pltpu
from jax.sharding import PartitionSpec as P

PERIOD = 12
LANES = 128
SUBLANES = 8
TOGETHER = 2
CORES = 2

credit_floor = 0.001
rollup_growth = 0.05
ALL = ("outer", "inner", "cell")

FEE, ACCOUNT, GUARANTEE, RATCHET, ROLLUP = range(5)
S_ACCOUNT, S_SURVIVING, S_GUARANTEE = range(3)


def lines_of(month, count):
    return slice(month * count, (month + 1) * count)


def parcel_kernel(outer_at, inner_at, premium, charge, mortality, fee_rate, sent, fees, received, scratch, in_sems, out_sems):
    each, wide = received.shape[1:]
    count = fees.shape[0]
    half = lax.rem(inner_at[0], CORES)
    copies = [pltpu.make_async_copy(fee_rate.at[half], fees, in_sems.at[0])]
    columns = pl.ds(pl.multiple_of(half * wide, wide), wide)
    for i, source in enumerate((premium, charge, mortality)):
        copies.append(pltpu.make_async_copy(source.at[:, columns], received.at[i], in_sems.at[i + 1]))
    for copy in copies:
        copy.start()
    for copy in copies:
        copy.wait()
    fee = fees[...]
    grow = jnp.log1p(-fee)
    per_fee = (1.0 - fee) / fee
    for r in range(each):
        for t in range(count):
            at = slice(t * LANES, (t + 1) * LANES)
            row = r * count + t
            scratch[row : row + 1, :] = received[0, r : r + 1, at] - received[1, r : r + 1, at]
            row = (each + r) * count + t
            scratch[row : row + 1, :] = received[2, r : r + 1, at]
    for r in range(each):
        at, then = lines_of(r, count), lines_of(each + r, count)
        month = (outer_at[0] * each + r).astype(jnp.float32)
        scratch[at, :] = scratch[at, :] * (fee * jnp.exp(-(month + 1.0) * grow))
        scratch[then, :] = scratch[then, :] * per_fee
    copies = [pltpu.make_async_copy(scratch, sent.at[i], out_sems.at[i]) for i in range(sent.shape[0])]
    for copy in copies:
        copy.start()
    for copy in copies:
        copy.wait()


def prepare_kernel(
    inner_at, lapse_table, lapse_index, kind, account, guarantee, fee_rate, cells, level, low, high, lapse, indices
):
    half = lax.rem(inner_at[0], CORES)
    for part, source in enumerate((half, 1 - half)):
        at = lines_of(part, kind.shape[1])
        cells[FEE, at, :] = fee_rate[source]
        cells[ACCOUNT, at, :] = account[source]
        cells[GUARANTEE, at, :] = guarantee[source]
        cells[RATCHET, at, :] = jnp.where(kind[source] == 1, 1.0, 0.0)
        cells[ROLLUP, at, :] = jnp.where(kind[source] == 2, 1.0, 0.0)
        indices[at, :] = lapse_index[source]
    fee, index = cells[FEE], indices[...]
    count = fee.shape[0]
    grow = jnp.log1p(-fee)
    per_fee = (1.0 - fee) / fee
    tables, months = lapse_table.shape

    def one_month(m, carry):
        at = pl.ds(pl.multiple_of(m * count, count), count)
        growth = jnp.exp(-(m.astype(jnp.float32) + 1.0) * grow)
        value = fee * growth
        level[at, :] = value
        low[at, :] = 0.5 * value
        high[at, :] = 1.5 * value
        base = jnp.full(fee.shape, lapse_table[0, m], jnp.float32)
        for k in range(1, tables):
            base = jnp.where(index == k, lapse_table[k, m], base)
        lapse[at, :] = base * (per_fee / growth)
        return carry

    lax.fori_loop(0, months, one_month, 0)


def second_table_kernel(own, near, far, across, rate, discount):
    first = own.shape[1] - rate.shape[0]
    lines = own.shape[0]
    for part, rates in enumerate((own[...], near[...], far[:lines, :], across[lines:, :])):
        at = slice(part * lines, (part + 1) * lines)
        discounting = jnp.exp(-rates)
        for m in range(rate.shape[0]):
            rate[m, at, :] = jnp.broadcast_to(rates[:, first + m : first + m + 1], (lines, LANES))
            discount[m, at, :] = jnp.broadcast_to(discounting[:, first + m : first + m + 1], (lines, LANES))


def world_year(start, part, plan, level, low, high, lapse, cells, state, credit):
    count = cells.shape[1]
    own = count // CORES
    each = plan.shape[1] // (2 * own)
    here = lines_of(part, own)
    fee, ratchet, rollup = cells[FEE, here, :], cells[RATCHET, here, :], cells[ROLLUP, here, :]
    kept = 1.0 - fee
    account, surviving, guarantee = state
    per_guarantee = 1.0 / guarantee
    for m in range(start, start + PERIOD):
        d, r = m // each, m % each
        at = slice(m * count + part * own, m * count + (part + 1) * own)
        flow = plan[d, lines_of(r, own), :]
        death = plan[d, lines_of(each + r, own), :]
        account = jnp.maximum(account + flow * per_guarantee, 0.0) * credit(m)
        bounded = jnp.minimum(jnp.maximum(account, low[at, :]), high[at, :])
        surviving = surviving * (kept - fee * death - lapse[at, :] * bounded)
        unit = level[at, :]
    growth = jnp.maximum(ratchet * (account / unit), 1.0 + rollup_growth * rollup)
    account = jnp.where(ratchet > 0.5, jnp.minimum(account, unit), account / growth)
    return account, surviving, guarantee * growth


def inner_paths(
    start, part, target, plan, level, low, high, lapse, cells, rows, credit, discount, kept_accounts, kept_growth, reserve,
    narrow=None,
):
    count = cells.shape[1]
    own = count // CORES
    each = plan.shape[1] // (2 * own)
    months, paths = credit.shape[:2]
    groups = paths // SUBLANES
    years = months // PERIOD
    full = (SUBLANES, LANES)

    def group(ref, m, g):
        return ref[m, SUBLANES * g : SUBLANES * (g + 1), :]

    def tiles_step(step, total, narrow=None):
        def of_paths(table, which, o, g):
            if narrow is None:
                return group(table, o, g)
            value = jnp.broadcast_to(narrow[which, SUBLANES * g : SUBLANES * (g + 1), o : o + 1], full)
            table[o, SUBLANES * g : SUBLANES * (g + 1), :] = value
            return value

        def spread_out(ref, i, m):
            return jnp.broadcast_to(ref[pl.ds(m * count + part * own + step * TOGETHER + i, 1), :], full)

        def of_cell(i, r):
            return jnp.broadcast_to(cells[r, pl.ds(part * own + step * TOGETHER + i, 1), :], full)

        def of_state(i, r):
            return jnp.broadcast_to(rows[r, pl.ds(step * TOGETHER + i, 1), :], full)

        def planned(i, m, second):
            d, r = m // each, m % each
            return jnp.broadcast_to(plan[d, pl.ds((r + second * each) * own + step * TOGETHER + i, 1), :], full)

        def of_tile(ref, i, m, g):
            return ref[i, m, SUBLANES * g : SUBLANES * (g + 1), :]

        def keep(ref, i, m, g, value):
            ref[i, m, SUBLANES * g : SUBLANES * (g + 1), :] = value

        tiles = range(TOGETHER)
        begin = [of_state(i, S_ACCOUNT) for i in tiles]
        base = [1.0 / of_state(i, S_GUARANTEE) for i in tiles]
        account = [[begin[i]] * groups for i in tiles]
        per_guarantee = [[base[i]] * groups for i in tiles]
        for o in range(months):
            flow = [planned(i, start + o, 0) for i in tiles]
            if o < PERIOD:
                flow = [flow[i] * base[i] for i in tiles]
            for g in range(groups):
                crediting = of_paths(credit, 0, o, g)
                for i in tiles:
                    term = flow[i] if o < PERIOD else flow[i] * per_guarantee[i][g]
                    account[i][g] = jnp.maximum(account[i][g] + term, 0.0) * crediting
                    keep(kept_accounts, i, o, g, account[i][g])
            if (o + 1) % PERIOD == 0 and o + 1 < months:
                y = o // PERIOD
                for i in tiles:
                    ratchet = of_cell(i, RATCHET)
                    grown = 1.0 + rollup_growth * of_cell(i, ROLLUP)
                    shrunk = 1.0 / grown
                    unit = spread_out(level, i, start + o)
                    per_unit = ratchet / unit
                    cap = jnp.where(ratchet > 0.5, unit, 1e30)
                    for g in range(groups):
                        growth = jnp.maximum(per_unit * account[i][g], grown)
                        keep(kept_growth, i, y, g, growth)
                        per_guarantee[i][g] = per_guarantee[i][g] / growth
                        account[i][g] = jnp.minimum(account[i][g], cap) * shrunk
                        keep(kept_growth, i, years + y, g, account[i][g])
        fee = [of_cell(i, FEE) for i in tiles]
        worth = [[None] * groups for i in tiles]
        for o in reversed(range(months)):
            m = start + o
            discounting = [None] * groups
            for i in tiles:
                unit, least, most = spread_out(level, i, m), spread_out(low, i, m), spread_out(high, i, m)
                lapsing = spread_out(lapse, i, m)
                death = planned(i, m, 1)
                staying = (1.0 - fee[i]) - fee[i] * death
                for g in range(groups):
                    after = of_tile(kept_accounts, i, o, g)
                    if o == 0:
                        before = begin[i]
                    elif o % PERIOD == 0:
                        before = of_tile(kept_growth, i, years + o // PERIOD - 1, g)
                    else:
                        before = of_tile(kept_accounts, i, o - 1, g)
                    value = death * jnp.maximum(unit - after, 0.0) - before
                    if worth[i][g] is not None:
                        later = worth[i][g]
                        if (o + 1) % PERIOD == 0:
                            later = later * of_tile(kept_growth, i, o // PERIOD, g)
                        bounded = jnp.minimum(jnp.maximum(after, least), most)
                        value = value + (staying - lapsing * bounded) * later
                    if i == 0:
                        discounting[g] = of_paths(discount, 1, o, g)
                    worth[i][g] = value * discounting[g]
        for i in tiles:
            summed = worth[i][0]
            for g in range(1, groups):
                summed = summed + worth[i][g]
            scale = of_state(i, S_GUARANTEE) * of_state(i, S_SURVIVING) * (1.0 / paths)
            row = jnp.sum(summed * scale, axis=0, keepdims=True)
            at = pl.multiple_of((target + step * TOGETHER + i) * LANES, LANES)
            reserve[0:1, pl.ds(at, LANES)] = row
            total = total + row
        return total

    total = jnp.zeros((1, LANES), jnp.float32)
    if narrow is not None:
        total = tiles_step(0, total, narrow)
    return lax.fori_loop(0 if narrow is None else 1, own // TOGETHER, tiles_step, total)


def block_sums(value, parts, block_hot):
    parts[...] = jnp.zeros_like(parts)
    for part in range(3):
        rounded = value.astype(jnp.bfloat16).astype(jnp.float32)
        parts[part : part + 1, :] = rounded
        value = value - rounded
    sums = jnp.dot(parts[...].astype(jnp.bfloat16), block_hot[...], preferred_element_type=jnp.float32)
    return sums[0:1, :] + sums[1:2, :] + sums[2:3, :]


def first_half(part, inner_at, world, spread, plan, level, low, high, lapse, cells, credit, discount, reserve, rows, kept_accounts, kept_growth, narrow=None):
    own = cells.shape[1] // CORES
    at, here = inner_at[0], lines_of(part, own)
    half = lax.rem(at, CORES)
    fee, guarantee = cells[FEE, here, :], cells[GUARANTEE, here, :]
    account = fee * cells[ACCOUNT, here, :] / guarantee
    state = (account, jnp.ones_like(account), guarantee)
    state = world_year(
        0, part, plan, level, low, high, lapse, cells, state,
        lambda m: 1.0 + jnp.maximum(world[at, m] - spread[at], credit_floor),
    )
    for r, value in enumerate(state):
        rows[r] = value
    target = (half if part == 0 else 1 - half) * own
    return inner_paths(
        PERIOD, part, target, plan, level, low, high, lapse, cells, rows, credit, discount, kept_accounts, kept_growth, reserve, narrow
    )


def first_own_kernel(
    inner_at, world, spread, plan, level, low, high, lapse, cells, own_rates, near_rates, far_rates, across_rates,
    reserve, rows, total, credit, discount, kept_accounts, kept_growth, narrow,
):
    lines = own_rates.shape[0]
    for part, rates in enumerate((own_rates[...], near_rates[...], far_rates[:lines, :], across_rates[lines:, :])):
        at = slice(part * lines, (part + 1) * lines)
        narrow[0, at, :] = 1.0 + jnp.maximum(rates - spread[inner_at[0]], credit_floor)
        narrow[1, at, :] = jnp.exp(-rates)
    total[...] = first_half(
        0, inner_at, world, spread, plan, level, low, high, lapse, cells, credit, discount, reserve, rows, kept_accounts, kept_growth, narrow
    )


def first_other_kernel(
    owners, inner_at, cell_at, world, spread, plan, level, low, high, lapse, cells, credit, discount,
    reserve_own, total_own, block_hot,
    reserve, rows, kept_here, next_one, next_two, next_three, kept_accounts, kept_growth, parts, shares,
):
    reserve[...] = reserve_own[...]
    total = total_own[...] + first_half(
        1, inner_at, world, spread, plan, level, low, high, lapse, cells, credit, discount, reserve, rows, kept_accounts, kept_growth
    )
    half = LANES // 2
    sums = block_sums(reserve[...], parts, block_hot)
    total = jnp.broadcast_to(jnp.sum(total, axis=1, keepdims=True), (1, half))
    for k in range(owners):
        shares[k : k + 1, :] = jnp.concatenate([sums[:, half * k : half * (k + 1)], total], axis=1)
    for s, target in enumerate((kept_here, next_one, next_two, next_three)):
        target[...] = shares[pl.ds(lax.rem(cell_at[0] + s, owners), 1), :]


def second_kernel(
    cells_all, inner_at, world, spread, place, kept_here, next_one, next_two, next_three,
    plan_own, plan_other, level, low, high, lapse, cells, rate, discount, rows_own, rows_other, reserve_one, block_hot,
    reserves, parcel, blocks_one, rows, reserve, credit, kept_accounts, kept_growth, parts,
):
    half = LANES // 2
    at = inner_at[0]
    own = cells.shape[1] // CORES
    whole = kept_here[...] + next_one[...] + next_two[...] + next_three[...]
    blocks_one[...] = whole
    spread_two = (spread[at] * (1.0 + jnp.tanh(whole / cells_all)))[0, half]
    for m in range(credit.shape[0]):
        credit[m] = 1.0 + jnp.maximum(rate[m] - spread_two, credit_floor)
    core = lax.rem(at, CORES)
    total = jnp.zeros((1, LANES), jnp.float32)
    for part, (plan, source) in enumerate(((plan_own, rows_own), (plan_other, rows_other))):
        state = world_year(
            PERIOD, part, plan, level, low, high, lapse, cells, tuple(source[r] for r in range(3)),
            lambda m: 1.0 + jnp.maximum(world[at, m] - spread_two, credit_floor),
        )
        for r, value in enumerate(state):
            rows[part, r] = value
    for part, plan in enumerate((plan_own, plan_other)):
        total = total + inner_paths(
            2 * PERIOD, part, (core if part == 0 else 1 - core) * own,
            plan, level, low, high, lapse, cells, rows.at[part], credit, discount, kept_accounts, kept_growth, reserve,
        )
    reserves[0] = reserve_one[...]
    reserves[1] = reserve[...]
    sums = block_sums(reserve[...], parts, block_hot)
    rate_sum = world[at, PERIOD]
    for m in range(PERIOD + 1, 2 * PERIOD):
        rate_sum = rate_sum + world[at, m]
    discount_world = jnp.exp(jnp.full((1, LANES), -rate_sum, jnp.float32))
    total_two = jnp.broadcast_to(jnp.sum(total, axis=1, keepdims=True), (1, LANES))
    loss = (discount_world * total_two - kept_here[...]) / cells_all
    lane = lax.broadcasted_iota(jnp.int32, (1, LANES), 1)
    loss = jnp.where(lane == half + place[0], loss, 0.0)
    for k in range(parcel.shape[1]):
        line = jnp.concatenate([sums[:, half * k : half * (k + 1)], loss[:, half:]], axis=1)
        parcel[:, k] = jnp.broadcast_to(line[None], (parcel.shape[0], 1, LANES))


def last_kernel(place, received, blocks_one, block_reserve, capital):
    outers, owners = received.shape[0], received.shape[1]
    half = LANES // 2
    losses = received[:, 0, 0, :]
    for k in range(1, owners):
        losses = losses + received[:, k, 0, :]
    lane = lax.broadcasted_iota(jnp.int32, losses.shape, 1) - half
    losses = jnp.where(lane >= 0, losses, 0.0)
    across = jnp.sum(losses, axis=0, keepdims=True)
    down = jnp.sum(losses, axis=1, keepdims=True)
    place_down = lax.broadcasted_iota(jnp.int32, losses.shape, 0)
    ahead = (across > down) | ((across == down) & (lane < place_down))
    ahead = ahead & (lane >= 0)
    rank = jnp.sum(jnp.where(ahead, 1.0, 0.0), axis=1, keepdims=True)
    count_top = outers // 4
    chosen = jnp.where(rank < count_top - 0.5, down, 0.0)
    capital[...] = jnp.broadcast_to(jnp.sum(chosen, axis=0, keepdims=True) / count_top, capital.shape)
    blocks = received[place[0], 0]
    for k in range(1, owners):
        blocks = blocks + received[place[0], k]
    block_reserve[0] = blocks_one[:, :half]
    block_reserve[1] = blocks[:, :half]


VMEM = pl.BlockSpec(memory_space=pltpu.VMEM)
SMEM = pl.BlockSpec(memory_space=pltpu.SMEM)
HBM = pl.BlockSpec(memory_space=pltpu.HBM)
MEBI = 1024 * 1024


def call(kernel, name, outs, specs, scratch=(), out_space=VMEM, limit=16, read=0):
    return pl.pallas_call(
        kernel,
        out_shape=outs,
        in_specs=specs,
        out_specs=jax.tree.map(lambda _: out_space, outs),
        scratch_shapes=list(scratch),
        compiler_params=pltpu.CompilerParams(vmem_limit_bytes=limit * MEBI),
        name=name,
        cost_estimate=pl.CostEstimate(flops=4000 * read, bytes_accessed=read, transcendentals=0),
    )


def floats(*lengths):
    return jax.ShapeDtypeStruct(lengths, jnp.float32)


def held(*lengths):
    return pltpu.VMEM(lengths, jnp.float32)


def body(
    premium,
    charge,
    mortality,
    lapse_table,
    lapse_index,
    guarantee_type,
    block_index,
    account_start,
    guarantee_start,
    fee_rate,
    first_rates,
    second_rates,
    world_rates,
    spread,
):
    outer_size, inner_size, cell_size = (lax.axis_size(a) for a in ALL)
    each, local = premium.shape
    months_all = each * outer_size
    paths = first_rates.shape[1] * inner_size
    months_one, months_two = first_rates.shape[2], second_rates.shape[2]
    cells_all = local * cell_size
    block_count = 4 * cells_all // LANES
    count = local // LANES
    own = count // CORES

    outer_at, inner_at, cell_at = (lax.axis_index(a).astype(jnp.int32) for a in ALL)
    place = (outer_at * inner_size + inner_at).reshape(1)
    outer_at, inner_one, cell_at = outer_at.reshape(1), inner_at.reshape(1), cell_at.reshape(1)

    def halves(value):
        return value.reshape(CORES, own, LANES)

    sent = call(
        parcel_kernel,
        "parcel",
        floats(outer_size, 2 * each * own, LANES),
        [SMEM] * 2 + [HBM] * 4,
        [
            held(own, LANES),
            held(3, each, own * LANES),
            held(2 * each * own, LANES),
            pltpu.SemaphoreType.DMA((4,)),
            pltpu.SemaphoreType.DMA((outer_size,)),
        ],
        HBM,
        60,
    )(outer_at, inner_one, premium, charge, mortality, halves(fee_rate))
    sent, first_rates, second_rates = lax.optimization_barrier((sent, first_rates, second_rates))
    rates = jnp.concatenate([first_rates, second_rates], axis=2)
    plan_own = lax.all_to_all(sent, "outer", 0, 0, tiled=True)
    own_rates, near_rates, far_rates, across_rates = (
        lax.dynamic_index_in_dim(rates, jnp.bitwise_xor(inner_at, s), 0, False) for s in range(inner_size)
    )
    far_rates = jnp.concatenate([far_rates, across_rates], axis=0)

    def swapped(value, s):
        return lax.ppermute(value, "inner", [(j, j ^ s) for j in range(inner_size)])

    far_rates = swapped(far_rates, CORES)
    near_rates = swapped(near_rates, 1)
    across_rates = swapped(far_rates, 1)
    shares = [own_rates, near_rates, far_rates, across_rates]
    coefs = [floats(5, count, LANES)] + [floats(months_all * count, LANES)] * 4
    cells, *coefs = call(prepare_kernel, "prepare", coefs, [SMEM] * 2 + [VMEM] * 5, [pltpu.VMEM((count, LANES), jnp.int32)], read=4 * MEBI)(
        inner_one,
        lapse_table,
        *(halves(a) for a in (lapse_index, guarantee_type, account_start, guarantee_start, fee_rate)),
    )
    block_hot = (block_index[:, None] == jnp.arange(block_count)[None, :]).astype(jnp.bfloat16)

    plan_other = swapped(plan_own, 1)

    def inner_scratch(months):
        return [
            held(TOGETHER, months, paths, LANES),
            held(TOGETHER, 2 * (months // PERIOD), paths, LANES),
        ]

    line = floats(1, LANES)
    state = floats(3, own, LANES)
    table = floats(months_one, paths, LANES)
    reserve_own, rows_own, total_own, credit_one, discount_one = call(
        first_own_kernel,
        "first_date_own",
        [floats(1, local), state, line, table, table],
        [SMEM] * 3 + [VMEM] * 10,
        inner_scratch(months_one) + [held(2, paths, months_one + months_two)],
        read=20 * MEBI,
    )(inner_one, world_rates, spread, plan_own, *coefs, cells, *shares)
    reserve_one, rows_other, kept_here, *others = call(
        functools.partial(first_other_kernel, cell_size),
        "first_date_other",
        [floats(1, local), state, line, line, line, line],
        [SMEM] * 4 + [VMEM] * 11,
        inner_scratch(months_one) + [held(SUBLANES, local), held(cell_size, LANES)],
    )(
        inner_one, cell_at, world_rates, spread, plan_other, *coefs, cells, credit_one, discount_one,
        reserve_own, total_own, block_hot,
    )

    others = [
        lax.ppermute(others[s - 1], "cell", [(k, (k + s) % cell_size) for k in range(cell_size)])
        for s in range(1, cell_size)
    ]
    reserve_one, *shares = lax.optimization_barrier((reserve_one, *shares))
    rate_two, discount_two = call(
        second_table_kernel, "second_tables", [floats(months_two, paths, LANES)] * 2, [VMEM] * 4
    )(*shares)

    reserves, parcel, blocks_one = call(
        functools.partial(second_kernel, cells_all),
        "second_date",
        [floats(2, 1, local), floats(outer_size * inner_size, cell_size, 1, LANES), line],
        [SMEM] * 4 + [VMEM] * 17,
        [held(CORES, 3, own, LANES), held(1, local), held(months_two, paths, LANES)]
        + inner_scratch(months_two)
        + [held(SUBLANES, local)],
    )(
        inner_one, world_rates, spread, place, kept_here, *others,
        plan_own, plan_other, *coefs, cells, rate_two, discount_two, rows_own, rows_other, reserve_one, block_hot,
    )

    received = lax.all_to_all(parcel.reshape(-1, 1, LANES), ALL, 0, 0, tiled=True)
    block_reserve, capital = call(
        last_kernel, "last_sums", [floats(2, 1, block_count // cell_size), line], [SMEM] + [VMEM] * 2
    )(place, received.reshape(parcel.shape), blocks_one)
    return reserves, block_reserve, capital[0, :1]


def solution(mesh):
    placed = (
        P("outer", "cell"),
        P("outer", "cell"),
        P("outer", "cell"),
        P(),
        P("cell"),
        P("cell"),
        P("cell"),
        P("cell"),
        P("cell"),
        P("cell"),
        P("outer", "inner", None),
        P("outer", "inner", None),
        P("outer", None),
        P("outer"),
    )
    return jax.shard_map(
        body,
        mesh=mesh,
        in_specs=placed,
        out_specs=(P(None, ("outer", "inner"), "cell"), P(None, ("outer", "inner"), "cell"), P()),
        check_vma=False,
    )
```

```python
import functools

import jax
import jax.numpy as jnp
from jax import lax
from jax.experimental import pallas as pl
from jax.experimental.pallas import tpu as pltpu
from jax.sharding import PartitionSpec as P

PERIOD = 12
LANES = 128
SUBLANES = 8
TOGETHER = 2
CORES = 2

credit_floor = 0.001
rollup_growth = 0.05
ALL = ("outer", "inner", "cell")

FEE, ACCOUNT, GUARANTEE, RATCHET, ROLLUP = range(5)
S_ACCOUNT, S_SURVIVING, S_GUARANTEE = range(3)


def lines_of(month, count):
    return slice(month * count, (month + 1) * count)


def parcel_kernel(outer_at, inner_at, premium, charge, mortality, fee_rate, sent, fees, received, scratch, in_sems, out_sems):
    each, wide = received.shape[1:]
    count = fees.shape[0]
    half = lax.rem(inner_at[0], CORES)
    copies = [pltpu.make_async_copy(fee_rate.at[half], fees, in_sems.at[0])]
    columns = pl.ds(pl.multiple_of(half * wide, wide), wide)
    for i, source in enumerate((premium, charge, mortality)):
        copies.append(pltpu.make_async_copy(source.at[:, columns], received.at[i], in_sems.at[i + 1]))
    for copy in copies:
        copy.start()
    for copy in copies:
        copy.wait()
    fee = fees[...]
    grow = jnp.log1p(-fee)
    per_fee = (1.0 - fee) / fee
    for r in range(each):
        for t in range(count):
            at = slice(t * LANES, (t + 1) * LANES)
            row = r * count + t
            scratch[row : row + 1, :] = received[0, r : r + 1, at] - received[1, r : r + 1, at]
            row = (each + r) * count + t
            scratch[row : row + 1, :] = received[2, r : r + 1, at]
    for r in range(each):
        at, then = lines_of(r, count), lines_of(each + r, count)
        month = (outer_at[0] * each + r).astype(jnp.float32)
        scratch[at, :] = scratch[at, :] * (fee * jnp.exp(-(month + 1.0) * grow))
        scratch[then, :] = scratch[then, :] * per_fee
    copies = [pltpu.make_async_copy(scratch, sent.at[i], out_sems.at[i]) for i in range(sent.shape[0])]
    for copy in copies:
        copy.start()
    for copy in copies:
        copy.wait()


def prepare_kernel(
    inner_at, lapse_table, lapse_index, kind, account, guarantee, fee_rate, rates,
    cells, level, low, high, lapse, rates_after, indices,
):
    rates_after[...] = rates[...]
    half = lax.rem(inner_at[0], CORES)
    for part, source in enumerate((half, 1 - half)):
        at = lines_of(part, kind.shape[1])
        cells[FEE, at, :] = fee_rate[source]
        cells[ACCOUNT, at, :] = account[source]
        cells[GUARANTEE, at, :] = guarantee[source]
        cells[RATCHET, at, :] = jnp.where(kind[source] == 1, 1.0, 0.0)
        cells[ROLLUP, at, :] = jnp.where(kind[source] == 2, 1.0, 0.0)
        indices[at, :] = lapse_index[source]
    fee, index = cells[FEE], indices[...]
    count = fee.shape[0]
    grow = jnp.log1p(-fee)
    per_fee = (1.0 - fee) / fee
    tables, months = lapse_table.shape

    def one_month(m, carry):
        at = pl.ds(pl.multiple_of(m * count, count), count)
        growth = jnp.exp(-(m.astype(jnp.float32) + 1.0) * grow)
        value = fee * growth
        level[at, :] = value
        low[at, :] = 0.5 * value
        high[at, :] = 1.5 * value
        base = jnp.full(fee.shape, lapse_table[0, m], jnp.float32)
        for k in range(1, tables):
            base = jnp.where(index == k, lapse_table[k, m], base)
        lapse[at, :] = base * (per_fee / growth)
        return carry

    lax.fori_loop(0, months, one_month, 0)


def second_table_kernel(own, near, far, across, rate, discount):
    first = own.shape[1] - rate.shape[0]
    lines = own.shape[0]
    for part, rates in enumerate((own[...], near[...], far[:lines, :], across[lines:, :])):
        at = slice(part * lines, (part + 1) * lines)
        discounting = jnp.exp(-rates)
        for m in range(rate.shape[0]):
            rate[m, at, :] = jnp.broadcast_to(rates[:, first + m : first + m + 1], (lines, LANES))
            discount[m, at, :] = jnp.broadcast_to(discounting[:, first + m : first + m + 1], (lines, LANES))


def world_year(start, part, plan, level, low, high, lapse, cells, state, credit):
    count = cells.shape[1]
    own = count // CORES
    each = plan.shape[1] // (2 * own)
    here = lines_of(part, own)
    fee, ratchet, rollup = cells[FEE, here, :], cells[RATCHET, here, :], cells[ROLLUP, here, :]
    kept = 1.0 - fee
    account, surviving, guarantee = state
    per_guarantee = 1.0 / guarantee
    for m in range(start, start + PERIOD):
        d, r = m // each, m % each
        at = slice(m * count + part * own, m * count + (part + 1) * own)
        flow = plan[d, lines_of(r, own), :]
        death = plan[d, lines_of(each + r, own), :]
        account = jnp.maximum(account + flow * per_guarantee, 0.0) * credit(m)
        bounded = jnp.minimum(jnp.maximum(account, low[at, :]), high[at, :])
        surviving = surviving * (kept - fee * death - lapse[at, :] * bounded)
        unit = level[at, :]
    growth = jnp.maximum(ratchet * (account / unit), 1.0 + rollup_growth * rollup)
    account = jnp.where(ratchet > 0.5, jnp.minimum(account, unit), account / growth)
    return account, surviving, guarantee * growth


def inner_paths(
    start, part, target, plan, level, low, high, lapse, cells, rows, credit, discount, kept_accounts, kept_growth, reserve,
    narrow=None,
):
    count = cells.shape[1]
    own = count // CORES
    each = plan.shape[1] // (2 * own)
    months, paths = credit.shape[:2]
    groups = paths // SUBLANES
    years = months // PERIOD
    full = (SUBLANES, LANES)

    def group(ref, m, g):
        return ref[m, SUBLANES * g : SUBLANES * (g + 1), :]

    def tiles_step(step, total, narrow=None):
        def of_paths(table, which, o, g):
            if narrow is None:
                return group(table, o, g)
            value = jnp.broadcast_to(narrow[which, SUBLANES * g : SUBLANES * (g + 1), o : o + 1], full)
            table[o, SUBLANES * g : SUBLANES * (g + 1), :] = value
            return value

        def spread_out(ref, i, m):
            return jnp.broadcast_to(ref[pl.ds(m * count + part * own + step * TOGETHER + i, 1), :], full)

        def of_cell(i, r):
            return jnp.broadcast_to(cells[r, pl.ds(part * own + step * TOGETHER + i, 1), :], full)

        def of_state(i, r):
            return jnp.broadcast_to(rows[r, pl.ds(step * TOGETHER + i, 1), :], full)

        def planned(i, m, second):
            d, r = m // each, m % each
            return jnp.broadcast_to(plan[d, pl.ds((r + second * each) * own + step * TOGETHER + i, 1), :], full)

        def of_tile(ref, i, m, g):
            return ref[i, m, SUBLANES * g : SUBLANES * (g + 1), :]

        def keep(ref, i, m, g, value):
            ref[i, m, SUBLANES * g : SUBLANES * (g + 1), :] = value

        tiles = range(TOGETHER)
        begin = [of_state(i, S_ACCOUNT) for i in tiles]
        base = [1.0 / of_state(i, S_GUARANTEE) for i in tiles]
        account = [[begin[i]] * groups for i in tiles]
        per_guarantee = [[base[i]] * groups for i in tiles]
        for o in range(months):
            flow = [planned(i, start + o, 0) for i in tiles]
            if o < PERIOD:
                flow = [flow[i] * base[i] for i in tiles]
            for g in range(groups):
                crediting = of_paths(credit, 0, o, g)
                for i in tiles:
                    term = flow[i] if o < PERIOD else flow[i] * per_guarantee[i][g]
                    account[i][g] = jnp.maximum(account[i][g] + term, 0.0) * crediting
                    keep(kept_accounts, i, o, g, account[i][g])
            if (o + 1) % PERIOD == 0 and o + 1 < months:
                y = o // PERIOD
                for i in tiles:
                    ratchet = of_cell(i, RATCHET)
                    grown = 1.0 + rollup_growth * of_cell(i, ROLLUP)
                    shrunk = 1.0 / grown
                    unit = spread_out(level, i, start + o)
                    per_unit = ratchet / unit
                    cap = jnp.where(ratchet > 0.5, unit, 1e30)
                    for g in range(groups):
                        growth = jnp.maximum(per_unit * account[i][g], grown)
                        keep(kept_growth, i, y, g, growth)
                        per_guarantee[i][g] = per_guarantee[i][g] / growth
                        account[i][g] = jnp.minimum(account[i][g], cap) * shrunk
                        keep(kept_growth, i, years + y, g, account[i][g])
        fee = [of_cell(i, FEE) for i in tiles]
        worth = [[None] * groups for i in tiles]
        for o in reversed(range(months)):
            m = start + o
            discounting = [None] * groups
            for i in tiles:
                unit, least, most = spread_out(level, i, m), spread_out(low, i, m), spread_out(high, i, m)
                lapsing = spread_out(lapse, i, m)
                death = planned(i, m, 1)
                staying = (1.0 - fee[i]) - fee[i] * death
                for g in range(groups):
                    after = of_tile(kept_accounts, i, o, g)
                    if o == 0:
                        before = begin[i]
                    elif o % PERIOD == 0:
                        before = of_tile(kept_growth, i, years + o // PERIOD - 1, g)
                    else:
                        before = of_tile(kept_accounts, i, o - 1, g)
                    value = death * jnp.maximum(unit - after, 0.0) - before
                    if worth[i][g] is not None:
                        later = worth[i][g]
                        if (o + 1) % PERIOD == 0:
                            later = later * of_tile(kept_growth, i, o // PERIOD, g)
                        bounded = jnp.minimum(jnp.maximum(after, least), most)
                        value = value + (staying - lapsing * bounded) * later
                    if i == 0:
                        discounting[g] = of_paths(discount, 1, o, g)
                    worth[i][g] = value * discounting[g]
        for i in tiles:
            summed = worth[i][0]
            for g in range(1, groups):
                summed = summed + worth[i][g]
            scale = of_state(i, S_GUARANTEE) * of_state(i, S_SURVIVING) * (1.0 / paths)
            row = jnp.sum(summed * scale, axis=0, keepdims=True)
            at = pl.multiple_of((target + step * TOGETHER + i) * LANES, LANES)
            reserve[0:1, pl.ds(at, LANES)] = row
            total = total + row
        return total

    total = jnp.zeros((1, LANES), jnp.float32)
    if narrow is not None:
        total = tiles_step(0, total, narrow)
    return lax.fori_loop(0 if narrow is None else 1, own // TOGETHER, tiles_step, total)


def block_sums(value, parts, block_hot):
    parts[...] = jnp.zeros_like(parts)
    for part in range(3):
        rounded = value.astype(jnp.bfloat16).astype(jnp.float32)
        parts[part : part + 1, :] = rounded
        value = value - rounded
    sums = jnp.dot(parts[...].astype(jnp.bfloat16), block_hot[...], preferred_element_type=jnp.float32)
    return sums[0:1, :] + sums[1:2, :] + sums[2:3, :]


def first_half(part, inner_at, world, spread, plan, level, low, high, lapse, cells, credit, discount, reserve, rows, kept_accounts, kept_growth, narrow=None):
    own = cells.shape[1] // CORES
    at, here = inner_at[0], lines_of(part, own)
    half = lax.rem(at, CORES)
    fee, guarantee = cells[FEE, here, :], cells[GUARANTEE, here, :]
    account = fee * cells[ACCOUNT, here, :] / guarantee
    state = (account, jnp.ones_like(account), guarantee)
    state = world_year(
        0, part, plan, level, low, high, lapse, cells, state,
        lambda m: 1.0 + jnp.maximum(world[at, m] - spread[at], credit_floor),
    )
    for r, value in enumerate(state):
        rows[r] = value
    target = (half if part == 0 else 1 - half) * own
    return inner_paths(
        PERIOD, part, target, plan, level, low, high, lapse, cells, rows, credit, discount, kept_accounts, kept_growth, reserve, narrow
    )


def first_own_kernel(
    inner_at, world, spread, plan, level, low, high, lapse, cells, own_rates, near_rates, far_rates, across_rates,
    reserve, rows, total, credit, discount, kept_accounts, kept_growth, narrow,
):
    lines = own_rates.shape[0]
    for part, rates in enumerate((own_rates[...], near_rates[...], far_rates[:lines, :], across_rates[lines:, :])):
        at = slice(part * lines, (part + 1) * lines)
        narrow[0, at, :] = 1.0 + jnp.maximum(rates - spread[inner_at[0]], credit_floor)
        narrow[1, at, :] = jnp.exp(-rates)
    total[...] = first_half(
        0, inner_at, world, spread, plan, level, low, high, lapse, cells, credit, discount, reserve, rows, kept_accounts, kept_growth, narrow
    )


def first_other_kernel(
    owners, inner_at, cell_at, world, spread, plan, level, low, high, lapse, cells, credit, discount,
    reserve_own, total_own, block_hot,
    reserve, rows, kept_here, next_one, next_two, next_three, kept_accounts, kept_growth, parts, shares,
):
    reserve[...] = reserve_own[...]
    total = total_own[...] + first_half(
        1, inner_at, world, spread, plan, level, low, high, lapse, cells, credit, discount, reserve, rows, kept_accounts, kept_growth
    )
    half = LANES // 2
    sums = block_sums(reserve[...], parts, block_hot)
    total = jnp.broadcast_to(jnp.sum(total, axis=1, keepdims=True), (1, half))
    for k in range(owners):
        shares[k : k + 1, :] = jnp.concatenate([sums[:, half * k : half * (k + 1)], total], axis=1)
    for s, target in enumerate((kept_here, next_one, next_two, next_three)):
        target[...] = shares[pl.ds(lax.rem(cell_at[0] + s, owners), 1), :]


def second_kernel(
    cells_all, inner_at, world, spread, place, kept_here, next_one, next_two, next_three,
    plan_own, plan_other, level, low, high, lapse, cells, rate, discount, rows_own, rows_other, reserve_one, block_hot,
    reserves, parcel, blocks_one, rows, reserve, credit, kept_accounts, kept_growth, parts,
):
    half = LANES // 2
    at = inner_at[0]
    own = cells.shape[1] // CORES
    whole = kept_here[...] + next_one[...] + next_two[...] + next_three[...]
    blocks_one[...] = whole
    spread_two = (spread[at] * (1.0 + jnp.tanh(whole / cells_all)))[0, half]
    for m in range(credit.shape[0]):
        credit[m] = 1.0 + jnp.maximum(rate[m] - spread_two, credit_floor)
    core = lax.rem(at, CORES)
    total = jnp.zeros((1, LANES), jnp.float32)
    for part, (plan, source) in enumerate(((plan_own, rows_own), (plan_other, rows_other))):
        state = world_year(
            PERIOD, part, plan, level, low, high, lapse, cells, tuple(source[r] for r in range(3)),
            lambda m: 1.0 + jnp.maximum(world[at, m] - spread_two, credit_floor),
        )
        for r, value in enumerate(state):
            rows[part, r] = value
    for part, plan in enumerate((plan_own, plan_other)):
        total = total + inner_paths(
            2 * PERIOD, part, (core if part == 0 else 1 - core) * own,
            plan, level, low, high, lapse, cells, rows.at[part], credit, discount, kept_accounts, kept_growth, reserve,
        )
    reserves[0] = reserve_one[...]
    reserves[1] = reserve[...]
    sums = block_sums(reserve[...], parts, block_hot)
    rate_sum = world[at, PERIOD]
    for m in range(PERIOD + 1, 2 * PERIOD):
        rate_sum = rate_sum + world[at, m]
    discount_world = jnp.exp(jnp.full((1, LANES), -rate_sum, jnp.float32))
    total_two = jnp.broadcast_to(jnp.sum(total, axis=1, keepdims=True), (1, LANES))
    loss = (discount_world * total_two - kept_here[...]) / cells_all
    lane = lax.broadcasted_iota(jnp.int32, (1, LANES), 1)
    loss = jnp.where(lane == half + place[0], loss, 0.0)
    lines = [
        jnp.concatenate([sums[:, half * k : half * (k + 1)], loss[:, half:]], axis=1) for k in range(sums.shape[1] // half)
    ]
    lines = jnp.concatenate(lines * (SUBLANES // len(lines)), axis=0)
    for at in range(0, parcel.shape[0], SUBLANES):
        parcel[at : at + SUBLANES, :] = lines


def last_kernel(owners, place, received, blocks_one, block_reserve, capital):
    half = LANES // 2
    outers = received.shape[0] // owners
    losses = received[pl.ds(0, outers, stride=owners), :]
    for k in range(1, owners):
        losses = losses + received[pl.ds(k, outers, stride=owners), :]
    lane = lax.broadcasted_iota(jnp.int32, losses.shape, 1) - half
    losses = jnp.where(lane >= 0, losses, 0.0)
    across = jnp.sum(losses, axis=0, keepdims=True)
    down = jnp.sum(losses, axis=1, keepdims=True)
    place_down = lax.broadcasted_iota(jnp.int32, losses.shape, 0)
    ahead = (across > down) | ((across == down) & (lane < place_down))
    ahead = ahead & (lane >= 0)
    rank = jnp.sum(jnp.where(ahead, 1.0, 0.0), axis=1, keepdims=True)
    count_top = outers // 4
    chosen = jnp.where(rank < count_top - 0.5, down, 0.0)
    capital[...] = jnp.broadcast_to(jnp.sum(chosen, axis=0, keepdims=True) / count_top, capital.shape)
    blocks = received[pl.ds(place[0] * owners, 1), :]
    for k in range(1, owners):
        blocks = blocks + received[pl.ds(place[0] * owners + k, 1), :]
    block_reserve[0] = blocks_one[:, :half]
    block_reserve[1] = blocks[:, :half]


VMEM = pl.BlockSpec(memory_space=pltpu.VMEM)
SMEM = pl.BlockSpec(memory_space=pltpu.SMEM)
HBM = pl.BlockSpec(memory_space=pltpu.HBM)
MEBI = 1024 * 1024


def call(kernel, name, outs, specs, scratch=(), out_space=VMEM, limit=16, read=0):
    return pl.pallas_call(
        kernel,
        out_shape=outs,
        in_specs=specs,
        out_specs=jax.tree.map(lambda _: out_space, outs),
        scratch_shapes=list(scratch),
        compiler_params=pltpu.CompilerParams(vmem_limit_bytes=limit * MEBI),
        name=name,
        cost_estimate=pl.CostEstimate(flops=4000 * read, bytes_accessed=read, transcendentals=0),
    )


def floats(*lengths):
    return jax.ShapeDtypeStruct(lengths, jnp.float32)


def held(*lengths):
    return pltpu.VMEM(lengths, jnp.float32)


def body(
    premium,
    charge,
    mortality,
    lapse_table,
    lapse_index,
    guarantee_type,
    block_index,
    account_start,
    guarantee_start,
    fee_rate,
    first_rates,
    second_rates,
    world_rates,
    spread,
):
    outer_size, inner_size, cell_size = (lax.axis_size(a) for a in ALL)
    each, local = premium.shape
    months_all = each * outer_size
    paths = first_rates.shape[1] * inner_size
    months_one, months_two = first_rates.shape[2], second_rates.shape[2]
    cells_all = local * cell_size
    block_count = 4 * cells_all // LANES
    count = local // LANES
    own = count // CORES

    outer_at, inner_at, cell_at = (lax.axis_index(a).astype(jnp.int32) for a in ALL)
    place = (outer_at * inner_size + inner_at).reshape(1)
    outer_at, inner_one, cell_at = outer_at.reshape(1), inner_at.reshape(1), cell_at.reshape(1)

    def halves(value):
        return value.reshape(CORES, own, LANES)

    sent = call(
        parcel_kernel,
        "parcel",
        floats(outer_size, 2 * each * own, LANES),
        [SMEM] * 2 + [HBM] * 4,
        [
            held(own, LANES),
            held(3, each, own * LANES),
            held(2 * each * own, LANES),
            pltpu.SemaphoreType.DMA((4,)),
            pltpu.SemaphoreType.DMA((outer_size,)),
        ],
        HBM,
        60,
    )(outer_at, inner_one, premium, charge, mortality, halves(fee_rate))
    sent, first_rates, second_rates = lax.optimization_barrier((sent, first_rates, second_rates))
    rates = jnp.concatenate([first_rates, second_rates], axis=2)
    plan_own = lax.all_to_all(sent, "outer", 0, 0, tiled=True)
    own_rates, near_rates, far_rates, across_rates = (
        lax.dynamic_index_in_dim(rates, jnp.bitwise_xor(inner_at, s), 0, False) for s in range(inner_size)
    )
    far_rates = jnp.concatenate([far_rates, across_rates], axis=0)

    def swapped(value, s):
        return lax.ppermute(value, "inner", [(j, j ^ s) for j in range(inner_size)])

    far_rates = swapped(far_rates, CORES)
    across_rates = swapped(far_rates, 1)
    coefs = [floats(5, count, LANES)] + [floats(months_all * count, LANES)] * 4
    coefs += [floats(*near_rates.shape)]
    cells, *coefs, near_rates = call(prepare_kernel, "prepare", coefs, [SMEM] * 2 + [VMEM] * 6, [pltpu.VMEM((count, LANES), jnp.int32)], read=4 * MEBI)(
        inner_one,
        lapse_table,
        *(halves(a) for a in (lapse_index, guarantee_type, account_start, guarantee_start, fee_rate)),
        near_rates,
    )
    near_rates = swapped(near_rates, 1)
    shares = [own_rates, near_rates, far_rates, across_rates]
    block_hot = (block_index[:, None] == jnp.arange(block_count)[None, :]).astype(jnp.bfloat16)

    plan_other = swapped(plan_own, 1)

    def inner_scratch(months):
        return [
            held(TOGETHER, months, paths, LANES),
            held(TOGETHER, 2 * (months // PERIOD), paths, LANES),
        ]

    line = floats(1, LANES)
    state = floats(3, own, LANES)
    table = floats(months_one, paths, LANES)
    reserve_own, rows_own, total_own, credit_one, discount_one = call(
        first_own_kernel,
        "first_date_own",
        [floats(1, local), state, line, table, table],
        [SMEM] * 3 + [VMEM] * 10,
        inner_scratch(months_one) + [held(2, paths, months_one + months_two)],
        read=20 * MEBI,
    )(inner_one, world_rates, spread, plan_own, *coefs, cells, *shares)
    reserve_one, rows_other, kept_here, *others = call(
        functools.partial(first_other_kernel, cell_size),
        "first_date_other",
        [floats(1, local), state, line, line, line, line],
        [SMEM] * 4 + [VMEM] * 11,
        inner_scratch(months_one) + [held(SUBLANES, local), held(cell_size, LANES)],
    )(
        inner_one, cell_at, world_rates, spread, plan_other, *coefs, cells, credit_one, discount_one,
        reserve_own, total_own, block_hot,
    )

    others = [
        lax.ppermute(others[s - 1], "cell", [(k, (k + s) % cell_size) for k in range(cell_size)])
        for s in range(1, cell_size)
    ]
    reserve_one, *shares = lax.optimization_barrier((reserve_one, *shares))
    rate_two, discount_two = call(
        second_table_kernel, "second_tables", [floats(months_two, paths, LANES)] * 2, [VMEM] * 4
    )(*shares)

    reserves, parcel, blocks_one = call(
        functools.partial(second_kernel, cells_all),
        "second_date",
        [floats(2, 1, local), floats(outer_size * inner_size * cell_size, LANES), line],
        [SMEM] * 4 + [VMEM] * 17,
        [held(CORES, 3, own, LANES), held(1, local), held(months_two, paths, LANES)]
        + inner_scratch(months_two)
        + [held(SUBLANES, local)],
    )(
        inner_one, world_rates, spread, place, kept_here, *others,
        plan_own, plan_other, *coefs, cells, rate_two, discount_two, rows_own, rows_other, reserve_one, block_hot,
    )

    received = lax.all_to_all(parcel, ALL, 0, 0, tiled=True)
    block_reserve, capital = call(
        functools.partial(last_kernel, cell_size), "last_sums", [floats(2, 1, block_count // cell_size), line], [SMEM] + [VMEM] * 2
    )(place, received, blocks_one)
    return reserves, block_reserve, capital[0, :1]


def solution(mesh):
    placed = (
        P("outer", "cell"),
        P("outer", "cell"),
        P("outer", "cell"),
        P(),
        P("cell"),
        P("cell"),
        P("cell"),
        P("cell"),
        P("cell"),
        P("cell"),
        P("outer", "inner", None),
        P("outer", "inner", None),
        P("outer", None),
        P("outer"),
    )
    return jax.shard_map(
        body,
        mesh=mesh,
        in_specs=placed,
        out_specs=(P(None, ("outer", "inner"), "cell"), P(None, ("outer", "inner"), "cell"), P()),
        check_vma=False,
    )
```

```python
import functools

import jax
import jax.numpy as jnp
from jax import lax
from jax.experimental import pallas as pl
from jax.experimental.pallas import tpu as pltpu
from jax.sharding import PartitionSpec as P

PERIOD = 12
LANES = 128
SUBLANES = 8
TOGETHER = 2
CORES = 2

credit_floor = 0.001
rollup_growth = 0.05
ALL = ("outer", "inner", "cell")

FEE, ACCOUNT, GUARANTEE, RATCHET, ROLLUP = range(5)
S_ACCOUNT, S_SURVIVING, S_GUARANTEE = range(3)


def lines_of(month, count):
    return slice(month * count, (month + 1) * count)


def parcel_kernel(outer_at, inner_at, premium, charge, mortality, fee_rate, sent, fees, received, scratch, in_sems, out_sems):
    each, wide = received.shape[1:]
    count = fees.shape[0]
    half = lax.rem(inner_at[0], CORES)
    copies = [pltpu.make_async_copy(fee_rate.at[half], fees, in_sems.at[0])]
    columns = pl.ds(pl.multiple_of(half * wide, wide), wide)
    for i, source in enumerate((premium, charge, mortality)):
        copies.append(pltpu.make_async_copy(source.at[:, columns], received.at[i], in_sems.at[i + 1]))
    for copy in copies:
        copy.start()
    copies[0].wait()
    fee = fees[...]
    grow = jnp.log1p(-fee)
    per_fee = (1.0 - fee) / fee
    scales = [fee * jnp.exp(-((outer_at[0] * each + r).astype(jnp.float32) + 1.0) * grow) for r in range(each)]
    for copy in copies[1:]:
        copy.wait()
    for r in range(each):
        for t in range(count):
            at = slice(t * LANES, (t + 1) * LANES)
            row = r * count + t
            scratch[row : row + 1, :] = received[0, r : r + 1, at] - received[1, r : r + 1, at]
            row = (each + r) * count + t
            scratch[row : row + 1, :] = received[2, r : r + 1, at]
    for r in range(each):
        at, then = lines_of(r, count), lines_of(each + r, count)
        scratch[at, :] = scratch[at, :] * scales[r]
        scratch[then, :] = scratch[then, :] * per_fee
    copies = [pltpu.make_async_copy(scratch, sent.at[i], out_sems.at[i]) for i in range(sent.shape[0])]
    for copy in copies:
        copy.start()
    for copy in copies:
        copy.wait()


def prepare_kernel(
    inner_at, lapse_table, lapse_index, kind, account, guarantee, fee_rate, rates,
    cells, level, low, high, lapse, rates_after, indices,
):
    rates_after[...] = rates[...]
    half = lax.rem(inner_at[0], CORES)
    for part, source in enumerate((half, 1 - half)):
        at = lines_of(part, kind.shape[1])
        cells[FEE, at, :] = fee_rate[source]
        cells[ACCOUNT, at, :] = account[source]
        cells[GUARANTEE, at, :] = guarantee[source]
        cells[RATCHET, at, :] = jnp.where(kind[source] == 1, 1.0, 0.0)
        cells[ROLLUP, at, :] = jnp.where(kind[source] == 2, 1.0, 0.0)
        indices[at, :] = lapse_index[source]
    fee, index = cells[FEE], indices[...]
    count = fee.shape[0]
    grow = jnp.log1p(-fee)
    per_fee = (1.0 - fee) / fee
    tables, months = lapse_table.shape

    def one_month(m, carry):
        at = pl.ds(pl.multiple_of(m * count, count), count)
        growth = jnp.exp(-(m.astype(jnp.float32) + 1.0) * grow)
        value = fee * growth
        level[at, :] = value
        low[at, :] = 0.5 * value
        high[at, :] = 1.5 * value
        base = jnp.full(fee.shape, lapse_table[0, m], jnp.float32)
        for k in range(1, tables):
            base = jnp.where(index == k, lapse_table[k, m], base)
        lapse[at, :] = base * (per_fee / growth)
        return carry

    lax.fori_loop(0, months, one_month, 0)


def second_table_kernel(own, near, far, across, rate, discount):
    first = own.shape[1] - rate.shape[0]
    lines = own.shape[0]
    for part, rates in enumerate((own[...], near[...], far[:lines, :], across[lines:, :])):
        at = slice(part * lines, (part + 1) * lines)
        discounting = jnp.exp(-rates)
        for m in range(rate.shape[0]):
            rate[m, at, :] = jnp.broadcast_to(rates[:, first + m : first + m + 1], (lines, LANES))
            discount[m, at, :] = jnp.broadcast_to(discounting[:, first + m : first + m + 1], (lines, LANES))


def world_year(start, part, plan, level, low, high, lapse, cells, state, credit):
    count = cells.shape[1]
    own = count // CORES
    each = plan.shape[1] // (2 * own)
    here = lines_of(part, own)
    fee, ratchet, rollup = cells[FEE, here, :], cells[RATCHET, here, :], cells[ROLLUP, here, :]
    kept = 1.0 - fee
    account, surviving, guarantee = state
    per_guarantee = 1.0 / guarantee
    for m in range(start, start + PERIOD):
        d, r = m // each, m % each
        at = slice(m * count + part * own, m * count + (part + 1) * own)
        flow = plan[d, lines_of(r, own), :]
        death = plan[d, lines_of(each + r, own), :]
        account = jnp.maximum(account + flow * per_guarantee, 0.0) * credit(m)
        bounded = jnp.minimum(jnp.maximum(account, low[at, :]), high[at, :])
        surviving = surviving * (kept - fee * death - lapse[at, :] * bounded)
        unit = level[at, :]
    growth = jnp.maximum(ratchet * (account / unit), 1.0 + rollup_growth * rollup)
    account = jnp.where(ratchet > 0.5, jnp.minimum(account, unit), account / growth)
    return account, surviving, guarantee * growth


def inner_paths(
    start, part, target, plan, level, low, high, lapse, cells, rows, credit, discount, kept_accounts, kept_growth, reserve,
    narrow=None,
):
    count = cells.shape[1]
    own = count // CORES
    each = plan.shape[1] // (2 * own)
    months, paths = credit.shape[:2]
    groups = paths // SUBLANES
    years = months // PERIOD
    full = (SUBLANES, LANES)

    def group(ref, m, g):
        return ref[m, SUBLANES * g : SUBLANES * (g + 1), :]

    def tiles_step(step, total, narrow=None):
        def of_paths(table, which, o, g):
            if narrow is None:
                return group(table, o, g)
            value = jnp.broadcast_to(narrow[which, SUBLANES * g : SUBLANES * (g + 1), o : o + 1], full)
            table[o, SUBLANES * g : SUBLANES * (g + 1), :] = value
            return value

        def spread_out(ref, i, m):
            return jnp.broadcast_to(ref[pl.ds(m * count + part * own + step * TOGETHER + i, 1), :], full)

        def of_cell(i, r):
            return jnp.broadcast_to(cells[r, pl.ds(part * own + step * TOGETHER + i, 1), :], full)

        def of_state(i, r):
            return jnp.broadcast_to(rows[r, pl.ds(step * TOGETHER + i, 1), :], full)

        def planned(i, m, second):
            d, r = m // each, m % each
            return jnp.broadcast_to(plan[d, pl.ds((r + second * each) * own + step * TOGETHER + i, 1), :], full)

        def of_tile(ref, i, m, g):
            return ref[i, m, SUBLANES * g : SUBLANES * (g + 1), :]

        def keep(ref, i, m, g, value):
            ref[i, m, SUBLANES * g : SUBLANES * (g + 1), :] = value

        tiles = range(TOGETHER)
        begin = [of_state(i, S_ACCOUNT) for i in tiles]
        base = [1.0 / of_state(i, S_GUARANTEE) for i in tiles]
        account = [[begin[i]] * groups for i in tiles]
        per_guarantee = [[base[i]] * groups for i in tiles]
        for o in range(months):
            flow = [planned(i, start + o, 0) for i in tiles]
            if o < PERIOD:
                flow = [flow[i] * base[i] for i in tiles]
            for g in range(groups):
                crediting = of_paths(credit, 0, o, g)
                for i in tiles:
                    term = flow[i] if o < PERIOD else flow[i] * per_guarantee[i][g]
                    account[i][g] = jnp.maximum(account[i][g] + term, 0.0) * crediting
                    keep(kept_accounts, i, o, g, account[i][g])
            if (o + 1) % PERIOD == 0 and o + 1 < months:
                y = o // PERIOD
                for i in tiles:
                    ratchet = of_cell(i, RATCHET)
                    grown = 1.0 + rollup_growth * of_cell(i, ROLLUP)
                    shrunk = 1.0 / grown
                    unit = spread_out(level, i, start + o)
                    per_unit = ratchet / unit
                    cap = jnp.where(ratchet > 0.5, unit, 1e30)
                    for g in range(groups):
                        growth = jnp.maximum(per_unit * account[i][g], grown)
                        keep(kept_growth, i, y, g, growth)
                        per_guarantee[i][g] = per_guarantee[i][g] / growth
                        account[i][g] = jnp.minimum(account[i][g], cap) * shrunk
                        keep(kept_growth, i, years + y, g, account[i][g])
        fee = [of_cell(i, FEE) for i in tiles]
        worth = [[None] * groups for i in tiles]
        for o in reversed(range(months)):
            m = start + o
            discounting = [None] * groups
            for i in tiles:
                unit, least, most = spread_out(level, i, m), spread_out(low, i, m), spread_out(high, i, m)
                lapsing = spread_out(lapse, i, m)
                death = planned(i, m, 1)
                staying = (1.0 - fee[i]) - fee[i] * death
                for g in range(groups):
                    after = of_tile(kept_accounts, i, o, g)
                    if o == 0:
                        before = begin[i]
                    elif o % PERIOD == 0:
                        before = of_tile(kept_growth, i, years + o // PERIOD - 1, g)
                    else:
                        before = of_tile(kept_accounts, i, o - 1, g)
                    value = death * jnp.maximum(unit - after, 0.0) - before
                    if worth[i][g] is not None:
                        later = worth[i][g]
                        if (o + 1) % PERIOD == 0:
                            later = later * of_tile(kept_growth, i, o // PERIOD, g)
                        bounded = jnp.minimum(jnp.maximum(after, least), most)
                        value = value + (staying - lapsing * bounded) * later
                    if i == 0:
                        discounting[g] = of_paths(discount, 1, o, g)
                    worth[i][g] = value * discounting[g]
        for i in tiles:
            summed = worth[i][0]
            for g in range(1, groups):
                summed = summed + worth[i][g]
            scale = of_state(i, S_GUARANTEE) * of_state(i, S_SURVIVING) * (1.0 / paths)
            row = jnp.sum(summed * scale, axis=0, keepdims=True)
            at = pl.multiple_of((target + step * TOGETHER + i) * LANES, LANES)
            reserve[0:1, pl.ds(at, LANES)] = row
            total = total + row
        return total

    total = jnp.zeros((1, LANES), jnp.float32)
    if narrow is not None:
        total = tiles_step(0, total, narrow)
    return lax.fori_loop(0 if narrow is None else 1, own // TOGETHER, tiles_step, total)


def block_sums(value, parts, block_hot):
    parts[...] = jnp.zeros_like(parts)
    for part in range(3):
        rounded = value.astype(jnp.bfloat16).astype(jnp.float32)
        parts[part : part + 1, :] = rounded
        value = value - rounded
    sums = jnp.dot(parts[...].astype(jnp.bfloat16), block_hot[...], preferred_element_type=jnp.float32)
    return sums[0:1, :] + sums[1:2, :] + sums[2:3, :]


def first_half(part, inner_at, world, spread, plan, level, low, high, lapse, cells, credit, discount, reserve, rows, kept_accounts, kept_growth, narrow=None):
    own = cells.shape[1] // CORES
    at, here = inner_at[0], lines_of(part, own)
    half = lax.rem(at, CORES)
    fee, guarantee = cells[FEE, here, :], cells[GUARANTEE, here, :]
    account = fee * cells[ACCOUNT, here, :] / guarantee
    state = (account, jnp.ones_like(account), guarantee)
    state = world_year(
        0, part, plan, level, low, high, lapse, cells, state,
        lambda m: 1.0 + jnp.maximum(world[at, m] - spread[at], credit_floor),
    )
    for r, value in enumerate(state):
        rows[r] = value
    target = (half if part == 0 else 1 - half) * own
    return inner_paths(
        PERIOD, part, target, plan, level, low, high, lapse, cells, rows, credit, discount, kept_accounts, kept_growth, reserve, narrow
    )


def first_own_kernel(
    inner_at, world, spread, plan, level, low, high, lapse, cells, own_rates, near_rates, far_rates, across_rates,
    reserve, rows, total, credit, discount, kept_accounts, kept_growth, narrow,
):
    lines = own_rates.shape[0]
    for part, rates in enumerate((own_rates[...], near_rates[...], far_rates[:lines, :], across_rates[lines:, :])):
        at = slice(part * lines, (part + 1) * lines)
        narrow[0, at, :] = 1.0 + jnp.maximum(rates - spread[inner_at[0]], credit_floor)
        narrow[1, at, :] = jnp.exp(-rates)
    total[...] = first_half(
        0, inner_at, world, spread, plan, level, low, high, lapse, cells, credit, discount, reserve, rows, kept_accounts, kept_growth, narrow
    )


def first_other_kernel(
    owners, inner_at, cell_at, world, spread, plan, level, low, high, lapse, cells, credit, discount,
    reserve_own, total_own, block_hot,
    reserve, rows, kept_here, next_one, next_two, next_three, kept_accounts, kept_growth, parts, shares,
):
    reserve[...] = reserve_own[...]
    total = total_own[...] + first_half(
        1, inner_at, world, spread, plan, level, low, high, lapse, cells, credit, discount, reserve, rows, kept_accounts, kept_growth
    )
    half = LANES // 2
    sums = block_sums(reserve[...], parts, block_hot)
    total = jnp.broadcast_to(jnp.sum(total, axis=1, keepdims=True), (1, half))
    for k in range(owners):
        shares[k : k + 1, :] = jnp.concatenate([sums[:, half * k : half * (k + 1)], total], axis=1)
    for s, target in enumerate((kept_here, next_one, next_two, next_three)):
        target[...] = shares[pl.ds(lax.rem(cell_at[0] + s, owners), 1), :]


def second_kernel(
    cells_all, inner_at, world, spread, place, kept_here, next_one, next_two, next_three,
    plan_own, plan_other, level, low, high, lapse, cells, rate, discount, rows_own, rows_other, reserve_one, block_hot,
    reserves, parcel, blocks_one, rows, reserve, credit, kept_accounts, kept_growth, parts,
):
    half = LANES // 2
    at = inner_at[0]
    own = cells.shape[1] // CORES
    whole = kept_here[...] + next_one[...] + next_two[...] + next_three[...]
    blocks_one[...] = whole
    spread_two = (spread[at] * (1.0 + jnp.tanh(whole / cells_all)))[0, half]
    for m in range(credit.shape[0]):
        credit[m] = 1.0 + jnp.maximum(rate[m] - spread_two, credit_floor)
    core = lax.rem(at, CORES)
    total = jnp.zeros((1, LANES), jnp.float32)
    for part, (plan, source) in enumerate(((plan_own, rows_own), (plan_other, rows_other))):
        state = world_year(
            PERIOD, part, plan, level, low, high, lapse, cells, tuple(source[r] for r in range(3)),
            lambda m: 1.0 + jnp.maximum(world[at, m] - spread_two, credit_floor),
        )
        for r, value in enumerate(state):
            rows[part, r] = value
    for part, plan in enumerate((plan_own, plan_other)):
        total = total + inner_paths(
            2 * PERIOD, part, (core if part == 0 else 1 - core) * own,
            plan, level, low, high, lapse, cells, rows.at[part], credit, discount, kept_accounts, kept_growth, reserve,
        )
    reserves[0] = reserve_one[...]
    reserves[1] = reserve[...]
    sums = block_sums(reserve[...], parts, block_hot)
    rate_sum = world[at, PERIOD]
    for m in range(PERIOD + 1, 2 * PERIOD):
        rate_sum = rate_sum + world[at, m]
    discount_world = jnp.exp(jnp.full((1, LANES), -rate_sum, jnp.float32))
    total_two = jnp.broadcast_to(jnp.sum(total, axis=1, keepdims=True), (1, LANES))
    loss = (discount_world * total_two - kept_here[...]) / cells_all
    lane = lax.broadcasted_iota(jnp.int32, (1, LANES), 1)
    loss = jnp.where(lane == half + place[0], loss, 0.0)
    lines = [
        jnp.concatenate([sums[:, half * k : half * (k + 1)], loss[:, half:]], axis=1) for k in range(sums.shape[1] // half)
    ]
    lines = jnp.concatenate(lines * (SUBLANES // len(lines)), axis=0)
    for at in range(0, parcel.shape[0], SUBLANES):
        parcel[at : at + SUBLANES, :] = lines


def last_kernel(owners, place, received, blocks_one, block_reserve, capital):
    half = LANES // 2
    outers = received.shape[0] // owners
    losses = received[pl.ds(0, outers, stride=owners), :]
    for k in range(1, owners):
        losses = losses + received[pl.ds(k, outers, stride=owners), :]
    lane = lax.broadcasted_iota(jnp.int32, losses.shape, 1) - half
    losses = jnp.where(lane >= 0, losses, 0.0)
    across = jnp.sum(losses, axis=0, keepdims=True)
    down = jnp.sum(losses, axis=1, keepdims=True)
    place_down = lax.broadcasted_iota(jnp.int32, losses.shape, 0)
    ahead = (across > down) | ((across == down) & (lane < place_down))
    ahead = ahead & (lane >= 0)
    rank = jnp.sum(jnp.where(ahead, 1.0, 0.0), axis=1, keepdims=True)
    count_top = outers // 4
    chosen = jnp.where(rank < count_top - 0.5, down, 0.0)
    capital[...] = jnp.broadcast_to(jnp.sum(chosen, axis=0, keepdims=True) / count_top, capital.shape)
    blocks = received[pl.ds(place[0] * owners, 1), :]
    for k in range(1, owners):
        blocks = blocks + received[pl.ds(place[0] * owners + k, 1), :]
    block_reserve[0] = blocks_one[:, :half]
    block_reserve[1] = blocks[:, :half]


VMEM = pl.BlockSpec(memory_space=pltpu.VMEM)
SMEM = pl.BlockSpec(memory_space=pltpu.SMEM)
HBM = pl.BlockSpec(memory_space=pltpu.HBM)
MEBI = 1024 * 1024


def call(kernel, name, outs, specs, scratch=(), out_space=VMEM, limit=16, read=0):
    return pl.pallas_call(
        kernel,
        out_shape=outs,
        in_specs=specs,
        out_specs=jax.tree.map(lambda _: out_space, outs),
        scratch_shapes=list(scratch),
        compiler_params=pltpu.CompilerParams(vmem_limit_bytes=limit * MEBI),
        name=name,
        cost_estimate=pl.CostEstimate(flops=4000 * read, bytes_accessed=read, transcendentals=0),
    )


def floats(*lengths):
    return jax.ShapeDtypeStruct(lengths, jnp.float32)


def held(*lengths):
    return pltpu.VMEM(lengths, jnp.float32)


def body(
    premium,
    charge,
    mortality,
    lapse_table,
    lapse_index,
    guarantee_type,
    block_index,
    account_start,
    guarantee_start,
    fee_rate,
    first_rates,
    second_rates,
    world_rates,
    spread,
):
    outer_size, inner_size, cell_size = (lax.axis_size(a) for a in ALL)
    each, local = premium.shape
    months_all = each * outer_size
    paths = first_rates.shape[1] * inner_size
    months_one, months_two = first_rates.shape[2], second_rates.shape[2]
    cells_all = local * cell_size
    block_count = 4 * cells_all // LANES
    count = local // LANES
    own = count // CORES

    outer_at, inner_at, cell_at = (lax.axis_index(a).astype(jnp.int32) for a in ALL)
    place = (outer_at * inner_size + inner_at).reshape(1)
    outer_at, inner_one, cell_at = outer_at.reshape(1), inner_at.reshape(1), cell_at.reshape(1)

    def halves(value):
        return value.reshape(CORES, own, LANES)

    sent = call(
        parcel_kernel,
        "parcel",
        floats(outer_size, 2 * each * own, LANES),
        [SMEM] * 2 + [HBM] * 4,
        [
            held(own, LANES),
            held(3, each, own * LANES),
            held(2 * each * own, LANES),
            pltpu.SemaphoreType.DMA((4,)),
            pltpu.SemaphoreType.DMA((outer_size,)),
        ],
        HBM,
        60,
    )(outer_at, inner_one, premium, charge, mortality, halves(fee_rate))
    sent, first_rates, second_rates = lax.optimization_barrier((sent, first_rates, second_rates))
    rates = jnp.concatenate([first_rates, second_rates], axis=2)
    plan_own = lax.all_to_all(sent, "outer", 0, 0, tiled=True)
    own_rates, near_rates, far_rates, across_rates = (
        lax.dynamic_index_in_dim(rates, jnp.bitwise_xor(inner_at, s), 0, False) for s in range(inner_size)
    )
    far_rates = jnp.concatenate([far_rates, across_rates], axis=0)

    def swapped(value, s):
        return lax.ppermute(value, "inner", [(j, j ^ s) for j in range(inner_size)])

    far_rates = swapped(far_rates, CORES)
    across_rates = swapped(far_rates, 1)
    coefs = [floats(5, count, LANES)] + [floats(months_all * count, LANES)] * 4
    coefs += [floats(*near_rates.shape)]
    cells, *coefs, near_rates = call(prepare_kernel, "prepare", coefs, [SMEM] * 2 + [VMEM] * 6, [pltpu.VMEM((count, LANES), jnp.int32)], read=4 * MEBI)(
        inner_one,
        lapse_table,
        *(halves(a) for a in (lapse_index, guarantee_type, account_start, guarantee_start, fee_rate)),
        near_rates,
    )
    near_rates = swapped(near_rates, 1)
    shares = [own_rates, near_rates, far_rates, across_rates]
    block_hot = (block_index[:, None] == jnp.arange(block_count)[None, :]).astype(jnp.bfloat16)

    plan_other = swapped(plan_own, 1)

    def inner_scratch(months):
        return [
            held(TOGETHER, months, paths, LANES),
            held(TOGETHER, 2 * (months // PERIOD), paths, LANES),
        ]

    line = floats(1, LANES)
    state = floats(3, own, LANES)
    table = floats(months_one, paths, LANES)
    reserve_own, rows_own, total_own, credit_one, discount_one = call(
        first_own_kernel,
        "first_date_own",
        [floats(1, local), state, line, table, table],
        [SMEM] * 3 + [VMEM] * 10,
        inner_scratch(months_one) + [held(2, paths, months_one + months_two)],
        read=20 * MEBI,
    )(inner_one, world_rates, spread, plan_own, *coefs, cells, *shares)
    reserve_one, rows_other, kept_here, *others = call(
        functools.partial(first_other_kernel, cell_size),
        "first_date_other",
        [floats(1, local), state, line, line, line, line],
        [SMEM] * 4 + [VMEM] * 11,
        inner_scratch(months_one) + [held(SUBLANES, local), held(cell_size, LANES)],
    )(
        inner_one, cell_at, world_rates, spread, plan_other, *coefs, cells, credit_one, discount_one,
        reserve_own, total_own, block_hot,
    )

    others = [
        lax.ppermute(others[s - 1], "cell", [(k, (k + s) % cell_size) for k in range(cell_size)])
        for s in range(1, cell_size)
    ]
    reserve_one, *shares = lax.optimization_barrier((reserve_one, *shares))
    rate_two, discount_two = call(
        second_table_kernel, "second_tables", [floats(months_two, paths, LANES)] * 2, [VMEM] * 4
    )(*shares)

    reserves, parcel, blocks_one = call(
        functools.partial(second_kernel, cells_all),
        "second_date",
        [floats(2, 1, local), floats(outer_size * inner_size * cell_size, LANES), line],
        [SMEM] * 4 + [VMEM] * 17,
        [held(CORES, 3, own, LANES), held(1, local), held(months_two, paths, LANES)]
        + inner_scratch(months_two)
        + [held(SUBLANES, local)],
    )(
        inner_one, world_rates, spread, place, kept_here, *others,
        plan_own, plan_other, *coefs, cells, rate_two, discount_two, rows_own, rows_other, reserve_one, block_hot,
    )

    received = lax.all_to_all(parcel, ALL, 0, 0, tiled=True)
    block_reserve, capital = call(
        functools.partial(last_kernel, cell_size), "last_sums", [floats(2, 1, block_count // cell_size), line], [SMEM] + [VMEM] * 2
    )(place, received, blocks_one)
    return reserves, block_reserve, capital[0, :1]


def solution(mesh):
    placed = (
        P("outer", "cell"),
        P("outer", "cell"),
        P("outer", "cell"),
        P(),
        P("cell"),
        P("cell"),
        P("cell"),
        P("cell"),
        P("cell"),
        P("cell"),
        P("outer", "inner", None),
        P("outer", "inner", None),
        P("outer", None),
        P("outer"),
    )
    return jax.shard_map(
        body,
        mesh=mesh,
        in_specs=placed,
        out_specs=(P(None, ("outer", "inner"), "cell"), P(None, ("outer", "inner"), "cell"), P()),
        check_vma=False,
    )
```
